256 devices in a mesh: walk: 32 (over y, x, core), grid: 8 (over z).
Axes of the slice: x: 4, y: 4, z: 8, core: 2. Of those that a mesh axis runs over, the one named last changes fastest.
Arguments:
- walkers_in: bfloat16 [32, 40, 40, 40, 128], P('walk', 'grid'), may hold values from -6 to 6
- trial: bfloat16 [40, 40, 40, 128], P('grid'), may hold values from -6 to 6
- fields: bfloat16 [2, 32, 40, 1600], P(None, 'walk', 'grid'), may hold values from -2.5 to 2.5
- sources: int32 [32], P('walk'), may hold values from 2 to 29, as said below
Outputs:
- walkers_out: bfloat16 [32, 40, 40, 40, 128], P('walk', 'grid')
- intersections: float32 [32, 64, 128], P('walk')
The draws below stay inside these ranges and needn't reach their ends.
Inputs may be any that keep to these rules, and one draw needn't show every extreme that they name: sources never falls with j; the device along walk that holds walker sources[j] is at most 2 indices away from the device of slot j, both limits reached in every draw.
All inputs are finite; a program needn't handle non-finite values.
Results may differ from the reference program's by a relative error of at most 0.029.
Values may be sent and summed in bfloat16 or wider, within the bound.
A program may use at most 64 MiB of HBM per device.

```python
import math
import jax
import jax.numpy as jnp
from jax import lax

G = 40
NORB = 64
W_DEV = 1
STEPS = 2
WALKERS = 32


def draw_sources(key, part):
    key = jax.random.fold_in(key, 7)
    lowest = 2 * W_DEV
    highest = WALKERS - 1 - 2 * W_DEV
    position = jnp.arange(WALKERS, dtype=jnp.int32)
    owner = position // W_DEV
    lower = jnp.maximum((owner - 2) * W_DEV, lowest)
    upper = jnp.minimum((owner + 3) * W_DEV - 1, highest)
    picked = jax.random.randint(key, (WALKERS,), lower, upper + 1, dtype=jnp.int32)
    picked = jnp.where(position == 0, lowest, picked)
    picked = jnp.where(position == WALKERS - 1, highest, picked)
    picked = lax.cummax(picked, axis=0)
    return picked.astype(jnp.int32)


def level_of(key, dims, split, least, high):
    level = 1.0
    for axis_at, parts in split:
        draws = jax.random.uniform(jax.random.fold_in(jax.random.fold_in(key, 6), axis_at), (parts,), jnp.float32, least / len(split), high / len(split))
        level = level * jnp.repeat(jnp.exp(draws), dims[axis_at] // parts).reshape((-1,) + (1,) * (len(dims) - 1 - axis_at))
    return level


def scatter_about(own_key, extent, width, reach, split=(), kind=jnp.bfloat16):
    result = jax.random.normal(own_key, extent, jnp.float32) * width
    if len(split) > 0:
        result = level_of(own_key, extent, split, -0.22, 0.18) * result
    return jnp.clip(result, min=-reach, max=reach).astype(kind)


def setup_inputs(seed: int = 0) -> dict:
    arg_keys = jax.random.split(jax.random.key(seed), 5)
    return {
        "walkers_in": scatter_about(arg_keys[0], (WALKERS, G, G, G, 2 * NORB), 1.0, 6.0, ((0, 32), (1, 8))),
        "trial": scatter_about(arg_keys[1], (G, G, G, 2 * NORB), 1.0, 6.0, ((0, 8),)),
        "fields": scatter_about(arg_keys[2], (STEPS, WALKERS, G, G * G), 0.4, 2.5, ((1, 32), (2, 8))),
        "sources": draw_sources(jax.random.fold_in(arg_keys[4], 71), 0),
    }


kinetic_rate = 0.001

def dft_matrix(points, sign):
    counter = jnp.arange(points, dtype=jnp.int32)
    phases = counter[:, None] * counter[None, :] % points
    angles = phases.astype(jnp.float32) * (2.0 * math.pi / points)
    cosine = jnp.cos(angles) / math.sqrt(points)
    sine_part = sign * jnp.sin(angles) / math.sqrt(points)
    matrix = jnp.stack([jnp.stack([cosine, sine_part], -1), jnp.stack([-sine_part, cosine], -1)], 1)
    return matrix.astype(jnp.bfloat16)

def damping(points, plane_rows):
    counter = jnp.arange(points, dtype=jnp.int32)
    signed = jnp.where(counter < points // 2, counter, counter - points).astype(jnp.float32)
    chosen = jnp.where(plane_rows < points // 2, plane_rows, plane_rows - points).astype(jnp.float32)
    total = chosen[:, None, None] ** 2 + signed[None, :, None] ** 2 + signed[None, None, :] ** 2
    return jnp.exp(-0.5 * kinetic_rate * total)

def along_z(block, matrix):
    return jnp.einsum('abcpo,cpwq->abwqo', block.astype(jnp.float32), matrix.astype(jnp.float32))

def along_y(block, matrix):
    return jnp.einsum('abcpo,bpwq->awcqo', block.astype(jnp.float32), matrix.astype(jnp.float32))

def along_x(block, matrix):
    return jnp.einsum('abcpo,apwq->wbcqo', block.astype(jnp.float32), matrix.astype(jnp.float32))

def propagate(orbitals_now, field_now):
    points = orbitals_now.shape[0]
    orbitals = orbitals_now.shape[3] // 2
    forward_table = dft_matrix(points, 1.0)
    backward_table = dft_matrix(points, -1.0)
    damp_factor = damping(points, jnp.arange(points, dtype=jnp.int32))[..., None, None]
    state = orbitals_now.astype(jnp.float32).reshape(points, points, points, 2, orbitals)
    for number in range(STEPS):
        scaled = (damp_factor * state).astype(jnp.bfloat16)
        section = along_z(scaled, forward_table).astype(jnp.bfloat16)
        section = along_y(section, forward_table).astype(jnp.bfloat16)
        real_space = along_x(section, forward_table)
        exponent = field_now[number].astype(jnp.float32).reshape(points, points, points).transpose(1, 0, 2)
        weighted = (real_space * jnp.exp(exponent)[..., None, None]).astype(jnp.bfloat16)
        section = along_x(weighted, backward_table).astype(jnp.bfloat16)
        section = along_y(section, backward_table).astype(jnp.bfloat16)
        state = damp_factor * along_z(section, backward_table)
    return state.astype(jnp.bfloat16).reshape(points, points, points, 2 * orbitals)

def reference(walkers_in, trial, fields, sources):
    points = walkers_in.shape[1]
    channels = walkers_in.shape[4]
    orbitals = channels // 2

    def single_walker(source):
        return propagate(walkers_in[source], fields[:, source])
    walkers_out = lax.map(single_walker, sources)
    flat_trial = trial.reshape(-1, channels)

    def intersection_one(walker):
        products = jnp.dot(flat_trial.T, walker.reshape(-1, channels), preferred_element_type=jnp.float32)
        real_part = products[:orbitals, :orbitals] + products[orbitals:, orbitals:]
        imag_part = products[:orbitals, orbitals:] - products[orbitals:, :orbitals]
        return jnp.concatenate([real_part, imag_part], axis=1) * (1.0 / math.sqrt(points ** 3))
    intersections = lax.map(intersection_one, walkers_out)
    return (walkers_out, intersections)
```

```python
import functools
import math

import jax
import jax.numpy as jnp
import ml_dtypes
import numpy as np
from jax import lax
from jax.experimental import pallas as pl
from jax.experimental.pallas import tpu as pltpu
from jax.sharding import PartitionSpec as P

MESH = pl.DeviceIdType.MESH
RATE = 0.001
G = 40
SLAB = 5
RING = 8
ORBS = 8
LOW = 8
HIGH = 5
LANES = 128
HALF = 64
BF = jnp.bfloat16
F32 = jnp.float32


def tables():
    n = np.arange(G)
    angle = (n[:, None] * n[None, :] % G) * (2.0 * math.pi / G)
    cos = (np.cos(angle) / math.sqrt(G)).astype(ml_dtypes.bfloat16).astype(np.float64)
    sin = (np.sin(angle) / math.sqrt(G)).astype(ml_dtypes.bfloat16).astype(np.float64)
    signed = np.where(n < G // 2, n, n - G)
    damp = np.exp(-0.5 * RATE * signed**2)
    fc, fs = cos.T * damp[None, :], sin.T * damp[None, :]
    bc, bs = damp[:, None] * cos.T, -damp[:, None] * sin.T
    both = (cos * damp[None, :] ** 2) @ cos.T + (sin * damp[None, :] ** 2) @ sin.T

    def left(parts, before, after):
        grown = [np.kron(np.kron(np.eye(before), p), np.eye(after)) for p in parts]
        return np.concatenate(grown, axis=0)

    def right(c, s):
        c4 = c.T.reshape(HIGH, LOW, HIGH, LOW)
        s4 = s.T.reshape(HIGH, LOW, HIGH, LOW)
        full = np.zeros((HIGH, 2, LOW, ORBS, HIGH, 2, LOW, ORBS))
        for o in range(ORBS):
            full[:, 0, :, o, :, 0, :, o] = c4
            full[:, 1, :, o, :, 1, :, o] = c4
            full[:, 0, :, o, :, 1, :, o] = s4
            full[:, 1, :, o, :, 0, :, o] = -s4
        return full.reshape(HIGH * LANES, HIGH * LANES)

    spread = np.zeros((2, RING, 16, HIGH, 2, LOW, ORBS))
    for step in range(2):
        for y in range(G):
            spread[step, y // SLAB, step * SLAB + y % SLAB, y // LOW, :, y % LOW, :] = 1.0
    zero = np.zeros_like(both)
    made = [
        left([fc, fs], SLAB, 1),
        left([both], SLAB, 1),
        left([bc, bs], SLAB, 1),
        left([fc, fs], 1, 8),
        left([both], 1, 8),
        left([bc, bs], 1, 8),
        right(fc, fs),
        right(both, zero),
        right(bc, bs),
        spread.reshape(2, RING * 16, HIGH * LANES),
    ]
    return [m.astype(ml_dtypes.bfloat16) for m in made]


def swap_blocks(parts, lane):
    parts = list(parts)
    for bit in range(3):
        shift = 8 << bit
        low = ((lane >> (3 + bit)) & 1) == 0
        for i in range(8):
            if not (i >> bit) & 1:
                j = i | (1 << bit)
                a, b = parts[i], parts[j]
                parts[i] = jnp.where(low, a, pltpu.roll(b, shift, 1))
                parts[j] = jnp.where(low, pltpu.roll(a, LANES - shift, 1), b)
    return parts


def kernel(
    sources, walker_hbm, trial_hbm, field_hbm,
    fz_h, kz_h, bz_h, fx_h, kx_h, bx_h, fy_h, ky_h, by_h, spread_h,
    out_hbm, inter_ref,
    whole, trial, sent, cand0, cand1, cand2, cand3, got, wa, wb, factor, back,
    late0, late1, late2, late3, late_odd, field, field_cand, field_all, field_t,
    fz, kz, bz, fx, kx, bx, fy, ky, by, spread, part, parts,
    load_sem, table_sem, in_send, in_recv, pre_send, pre_recv, back_send, back_recv,
    post_send, post_recv, f_send, f_recv, fz_send, fz_recv, sum_send, sum_recv, local_sem, out_sem,
):
    w = lax.axis_index("walk")
    me = lax.axis_index("grid")
    walks = lax.axis_size("walk")
    parity = lax.rem(me, 2)
    chosen = jnp.clip(sources[0] - w + 2, 0, 4)
    cands = (cand0, cand1, cand2, cand3)
    lates = (late0, late1, late2, late3)
    deltas = (1, -1, 2, -2)

    def ring(k):
        return lax.rem(me + k + RING, RING)

    def walk_at(delta):
        return (lax.rem(w + delta + walks, walks), me)

    def remote(src, dst, ssem, rsem, device):
        return pltpu.make_async_remote_copy(
            src_ref=src, dst_ref=dst, send_sem=ssem, recv_sem=rsem, device_id=device, device_id_type=MESH
        )

    load_w = pltpu.make_async_copy(walker_hbm.at[0], whole, load_sem.at[0])
    load_w.start()
    load_f = pltpu.make_async_copy(field_hbm, field, load_sem.at[1])
    load_f.start()
    load_t = pltpu.make_async_copy(trial_hbm, trial, load_sem.at[2])
    load_t.start()
    table_loads = []
    pairs = ((fz_h, fz), (kz_h, kz), (bz_h, bz), (fx_h, fx), (kx_h, kx), (bx_h, bx), (fy_h, fy), (ky_h, ky), (by_h, by),
             (spread_h, spread))
    for i, (src, dst) in enumerate(pairs):
        c = pltpu.make_async_copy(src, dst, table_sem.at[i])
        c.start()
        table_loads.append(c)

    barrier = pltpu.get_barrier_semaphore()
    for k in range(1, RING):
        pl.semaphore_signal(barrier, inc=1, device_id=(w, ring(k)), device_id_type=MESH)
    for delta in deltas:
        pl.semaphore_signal(barrier, inc=1, device_id=walk_at(delta), device_id_type=MESH)

    lane = lax.broadcasted_iota(jnp.int32, (G, LANES), 1)
    load_w.wait()

    def shuffle(u, _):
        x, yh = u // HIGH, lax.rem(u, HIGH)
        rows = [whole[x, yh * LOW + i].astype(F32) for i in range(LOW)]
        moved = swap_blocks(rows, lane)
        for d in range(RING):
            if d % 2 == 0:
                sent[d, x, yh] = moved[d].astype(BF)
            else:
                cands[d // 2][2, x, yh] = moved[d].astype(BF)
        return 0

    lax.fori_loop(0, SLAB * HIGH, shuffle, 0)
    load_f.wait()
    field_cand[2] = field[...]
    pl.semaphore_wait(barrier, RING - 1 + 4)

    def field_copy(i):
        return remote(field, field_cand.at[2 - deltas[i]], f_send.at[i], f_recv.at[2 - deltas[i]], walk_at(deltas[i]))

    for i in range(4):
        field_copy(i).start()

    def in_copy(d):
        return remote(sent.at[d], got.at[me], in_send.at[d], in_recv.at[me], (w, d))

    def self_in(d):
        return pltpu.make_async_copy(sent.at[d], got.at[d], local_sem.at[0])

    def send_in(d):
        @pl.when(d != me)
        def _():
            in_copy(d).start()

        @pl.when(d == me)
        def _():
            self_in(d).start()

    for k in range(RING):
        d = ring(k)

        @pl.when(lax.rem(d, 2) == 0)
        def _():
            send_in(d)

    def pre_copy(i, c):
        return remote(
            cands[c].at[2], cands[c].at[2 - deltas[i]], pre_send.at[i, c], pre_recv.at[2 - deltas[i], c], walk_at(deltas[i])
        )

    for c in range(4):
        for i in range(4):
            pre_copy(i, c).start()

    for i in range(4):
        field_copy(i).wait_recv()
    picked_field = field_cand[chosen]
    field_all[me] = jnp.where(parity == 0, field_cand[2].astype(F32), picked_field.astype(F32)).astype(BF)
    part_field = field_cand.at[5]
    part_field[...] = picked_field

    def ring_field(d, src):
        return remote(src, field_all.at[me], fz_send.at[d], fz_recv.at[me], (w, d))

    for k in range(1, RING):
        d = ring(k)

        @pl.when(lax.rem(d, 2) == 0)
        def _():
            ring_field(d, field).start()

        @pl.when(lax.rem(d, 2) == 1)
        def _():
            ring_field(d, part_field).start()

    for c in range(4):
        for i in range(4):
            pre_copy(i, c).wait_recv()

        def pick(u, _):
            sent[2 * c + 1, u] = cands[c][chosen, u]
            return 0

        lax.fori_loop(0, SLAB, pick, 0)
        send_in(jnp.int32(2 * c + 1))

    for k in range(1, RING):
        g = ring(k)
        remote(field, field_all.at[g], fz_send.at[g], fz_recv.at[g], (w, g)).wait_recv()
    for c in table_loads:
        c.wait()
    for i in range(RING):
        field_t[:, i * 16:(i + 1) * 16] = field_all[i].astype(F32).T

    for step in range(2):
        def spread_out(i, _):
            rows = field_t[pl.ds(i * 400, 400), :].astype(BF)
            grown = jnp.exp(jnp.dot(rows, spread[step], preferred_element_type=F32))
            for yh in range(HIGH):
                factor[step, pl.ds(i * 10, 10), yh] = grown[:, yh * LANES:(yh + 1) * LANES].reshape(10, G, LANES)
            return 0

        lax.fori_loop(0, 4, spread_out, 0)

    for k in range(1, RING):
        g = ring(k)
        remote(sent.at[g], got.at[g], in_send.at[g], in_recv.at[g], (w, g)).wait_recv()
    self_in(me).wait()

    sign = jnp.where(lax.broadcasted_iota(jnp.int32, (1, LANES), 1) < HALF, -1.0, 1.0).astype(F32)

    def cols(value, yh):
        return value[:, yh * LANES:(yh + 1) * LANES]

    def combined(value, yh, rows):
        c, s = cols(value, yh)[:rows], cols(value, yh)[rows:]
        return c + pltpu.roll(s, HALF, 1) * sign

    def stage_fz(g, _):
        data = [got[g, :, yh].astype(F32).reshape(200, LANES).astype(BF) for yh in range(HIGH)]
        value = jnp.dot(fz[...], jnp.concatenate(data, axis=1), preferred_element_type=F32)
        for yh in range(HIGH):
            wa[pl.ds(g * SLAB, SLAB), yh] = combined(value, yh, 200).reshape(SLAB, G, LANES)
        return 0

    lax.fori_loop(0, RING, stage_fz, 0)

    def stage_fy(i, _):
        data = [wa[pl.ds(i * 10, 10), yh].reshape(400, LANES).astype(BF) for yh in range(HIGH)]
        value = jnp.dot(jnp.concatenate(data, axis=1), fy[...], preferred_element_type=F32)
        for yh in range(HIGH):
            wb[pl.ds(i * 10, 10), yh] = cols(value, yh).reshape(10, G, LANES)
        return 0

    lax.fori_loop(0, 4, stage_fy, 0)

    def stage_fx(i, _):
        at = pl.ds(pl.multiple_of(i * 8, 8), 8)
        data = [wb[:, yh, at].reshape(320, LANES).astype(BF) for yh in range(HIGH)]
        value = jnp.dot(fx[...], jnp.concatenate(data, axis=1), preferred_element_type=F32)
        lit = [
            (combined(value, yh, 320) * factor[0, :, yh, at].reshape(320, LANES)).astype(BF) for yh in range(HIGH)
        ]
        value = jnp.dot(kx[...], jnp.concatenate(lit, axis=1), preferred_element_type=F32)
        for yh in range(HIGH):
            wa[:, yh, at] = cols(value, yh).reshape(G, 8, LANES)
        return 0

    lax.fori_loop(0, 5, stage_fx, 0)

    def stage_kz(g, _):
        data = [wa[pl.ds(g * SLAB, SLAB), yh].reshape(200, LANES).astype(BF) for yh in range(HIGH)]
        value = jnp.dot(kz[...], jnp.concatenate(data, axis=1), preferred_element_type=F32)
        for yh in range(HIGH):
            wb[pl.ds(g * SLAB, SLAB), yh] = cols(value, yh).reshape(SLAB, G, LANES)
        return 0

    lax.fori_loop(0, RING, stage_kz, 0)

    def stage_ky(i, _):
        data = [wb[pl.ds(i * 10, 10), yh].reshape(400, LANES).astype(BF) for yh in range(HIGH)]
        value = jnp.dot(jnp.concatenate(data, axis=1), ky[...], preferred_element_type=F32)
        lit = [
            (cols(value, yh) * factor[1, pl.ds(i * 10, 10), yh].reshape(400, LANES)).astype(BF) for yh in range(HIGH)
        ]
        value = jnp.dot(jnp.concatenate(lit, axis=1), by[...], preferred_element_type=F32)
        for yh in range(HIGH):
            wa[pl.ds(i * 10, 10), yh] = cols(value, yh).reshape(10, G, LANES)
        return 0

    lax.fori_loop(0, 4, stage_ky, 0)

    def stage_bx(i, _):
        at = pl.ds(pl.multiple_of(i * 8, 8), 8)
        data = [wa[:, yh, at].reshape(320, LANES).astype(BF) for yh in range(HIGH)]
        value = jnp.dot(bx[...], jnp.concatenate(data, axis=1), preferred_element_type=F32)
        for yh in range(HIGH):
            wb[:, yh, at] = combined(value, yh, 320).reshape(G, 8, LANES)
        return 0

    lax.fori_loop(0, 5, stage_bx, 0)

    def back_copy(d, g):
        here = lates[d // 2].at[2] if d % 2 == 0 else late_odd.at[d // 2]
        return remote(back.at[g], here, back_send.at[g], back_recv.at[d], (w, g))

    def self_back(d):
        here = lates[d // 2].at[2] if d % 2 == 0 else late_odd.at[d // 2]
        return pltpu.make_async_copy(back.at[d], here, local_sem.at[1])

    def send_back(g):
        for d in range(RING):
            @pl.when(jnp.logical_and(d == me, g != me))
            def _():
                back_copy(d, g).start()

            @pl.when(jnp.logical_and(d == me, g == me))
            def _():
                self_back(d).start()

    def stage_bz(i, _):
        g = lax.rem(me + i + 1, RING)
        data = [wb[pl.ds(g * SLAB, SLAB), yh].reshape(200, LANES).astype(BF) for yh in range(HIGH)]
        value = jnp.dot(bz[...], jnp.concatenate(data, axis=1), preferred_element_type=F32)
        for yh in range(HIGH):
            back[g, :, yh] = combined(value, yh, 200).reshape(SLAB, G, LANES).astype(BF)

        send_back(g)
        return 0

    lax.fori_loop(0, RING, stage_bz, 0)

    def back_arrival(d):
        @pl.when(d != me)
        def _():
            back_copy(d, jnp.int32(d)).wait_recv()

        @pl.when(d == me)
        def _():
            self_back(d).wait()

    def post_copy(i, c):
        return remote(
            lates[c].at[2], lates[c].at[2 - deltas[i]], post_send.at[i, c], post_recv.at[2 - deltas[i], c], walk_at(deltas[i])
        )

    for c in range(4):
        back_arrival(2 * c)
        for i in range(4):
            post_copy(i, c).start()
    for c in range(4):
        back_arrival(2 * c + 1)
    for c in range(4):
        for i in range(4):
            post_copy(i, c).wait_recv()

    load_t.wait()
    part[...] = jnp.zeros_like(part)

    def finish(u, _):
        x, yh = u // HIGH, lax.rem(u, HIGH)
        rows = []
        for d in range(RING):
            if d % 2 == 0:
                rows.append(lates[d // 2][chosen, x, yh].astype(F32))
            else:
                rows.append(late_odd[d // 2, x, yh].astype(F32))
        moved = swap_blocks(rows, lane)
        for i in range(LOW):
            whole[x, yh * LOW + i] = moved[i].astype(BF)
        new = jnp.concatenate(moved, axis=0).astype(BF)
        old = trial[x, pl.ds(yh * LOW, LOW)].astype(F32).reshape(LOW * G, LANES).astype(BF)
        part[...] += lax.dot_general(old, new, (((0,), (0,)), ((), ())), preferred_element_type=F32)
        return 0

    lax.fori_loop(0, SLAB * HIGH, finish, 0)
    store = pltpu.make_async_copy(whole, out_hbm.at[0], out_sem)
    store.start()

    lower = part[HALF:, :]
    mine = part[:HALF, :] - pltpu.roll(lower, HALF, 1) * sign
    parts[me] = mine.astype(BF)

    def sum_copy(d):
        return remote(parts.at[me], parts.at[me], sum_send.at[d], sum_recv.at[me], (w, d))

    for k in range(1, RING):
        sum_copy(ring(k)).start()
    for k in range(1, RING):
        g = ring(k)
        remote(parts.at[g], parts.at[g], sum_send.at[g], sum_recv.at[g], (w, g)).wait_recv()
    total = parts[0].astype(F32)
    for g in range(1, RING):
        total = total + parts[g].astype(F32)
    inter_ref[...] = total * (1.0 / math.sqrt(G**3))

    for k in range(1, RING):
        d = ring(k)
        in_copy(d).wait_send()
        ring_field(d, field).wait_send()
        back_copy(0, d).wait_send()
        sum_copy(d).wait_send()
    for i in range(4):
        field_copy(i).wait_send()
        for c in range(4):
            pre_copy(i, c).wait_send()
            post_copy(i, c).wait_send()
    store.wait()


def on_device(walkers_in, trial, fields, sources):
    made = [jnp.asarray(t) for t in tables()]
    field = jnp.pad(fields.reshape(2 * SLAB, G * G), ((0, 16 - 2 * SLAB), (0, 0)))
    anywhere = pl.BlockSpec(memory_space=pl.ANY)
    chunk = (SLAB, HIGH, G, LANES)
    dma = pltpu.SemaphoreType.DMA
    scratch = [
        pltpu.VMEM((SLAB, G, G, LANES), BF),
        pltpu.VMEM((SLAB, G, G, LANES), BF),
        pltpu.VMEM((RING,) + chunk, BF),
        *[pltpu.VMEM((5,) + chunk, BF) for _ in range(4)],
        pltpu.VMEM((RING,) + chunk, BF),
        pltpu.VMEM((G, HIGH, G, LANES), F32),
        pltpu.VMEM((G, HIGH, G, LANES), F32),
        pltpu.VMEM((2, G, HIGH, G, LANES), F32),
        pltpu.VMEM((RING,) + chunk, BF),
        *[pltpu.VMEM((5,) + chunk, BF) for _ in range(4)],
        pltpu.VMEM((4,) + chunk, BF),
        pltpu.VMEM((16, G * G), BF),
        pltpu.VMEM((6, 16, G * G), BF),
        pltpu.VMEM((RING, 16, G * G), BF),
        pltpu.VMEM((G * G, RING * 16), F32),
    ]
    scratch += [pltpu.VMEM(t.shape, BF) for t in made]
    scratch += [pltpu.VMEM((LANES, LANES), F32), pltpu.VMEM((RING, HALF, LANES), BF)]
    scratch += [
        dma((3,)), dma((len(made),)), dma((RING,)), dma((RING,)), dma((4, 4)), dma((5, 4)), dma((RING,)), dma((RING,)),
        dma((4, 4)), dma((5, 4)), dma((4,)), dma((5,)), dma((RING,)), dma((RING,)), dma((RING,)), dma((RING,)),
        dma((2,)), dma,
    ]


    walkers_out, inter = pl.pallas_call(
        kernel,
        out_shape=(
            jax.ShapeDtypeStruct((1, SLAB, G, G, LANES), BF),
            jax.ShapeDtypeStruct((HALF, LANES), F32),
        ),
        in_specs=[pl.BlockSpec(memory_space=pltpu.SMEM)] + [anywhere] * (3 + len(made)),
        out_specs=(anywhere, pl.BlockSpec(memory_space=pltpu.VMEM)),
        scratch_shapes=scratch,
        compiler_params=pltpu.CompilerParams(
            collective_id=0, has_side_effects=True, vmem_limit_bytes=62 * 2**20
        ),
        name="walkers",
    )(sources, walkers_in, trial, field, *made)
    return walkers_out, inter[None]


def solution(mesh):
    placed = (
        P("walk", "grid", None, None, None),
        P("grid", None, None, None),
        P(None, "walk", "grid", None),
        P("walk"),
    )
    return jax.shard_map(
        on_device,
        mesh=mesh,
        in_specs=placed,
        out_specs=(P("walk", "grid", None, None, None), P("walk", None, None)),
        check_vma=False,
    )
```

```python
import functools
import math

import jax
import jax.numpy as jnp
import ml_dtypes
import numpy as np
from jax import lax
from jax.experimental import pallas as pl
from jax.experimental.pallas import tpu as pltpu
from jax.sharding import PartitionSpec as P

MESH = pl.DeviceIdType.MESH
RATE = 0.001
G = 40
SLAB = 5
RING = 8
ORBS = 8
LOW = 8
HIGH = 5
LANES = 128
HALF = 64
BF = jnp.bfloat16
F32 = jnp.float32


def tables():
    n = np.arange(G)
    angle = (n[:, None] * n[None, :] % G) * (2.0 * math.pi / G)
    cos = (np.cos(angle) / math.sqrt(G)).astype(ml_dtypes.bfloat16).astype(np.float64)
    sin = (np.sin(angle) / math.sqrt(G)).astype(ml_dtypes.bfloat16).astype(np.float64)
    signed = np.where(n < G // 2, n, n - G)
    damp = np.exp(-0.5 * RATE * signed**2)
    fc, fs = cos.T * damp[None, :], sin.T * damp[None, :]
    bc, bs = damp[:, None] * cos.T, -damp[:, None] * sin.T
    both = (cos * damp[None, :] ** 2) @ cos.T + (sin * damp[None, :] ** 2) @ sin.T

    def left(parts, before, after):
        grown = [np.kron(np.kron(np.eye(before), p), np.eye(after)) for p in parts]
        return np.concatenate(grown, axis=0)

    def right(c, s):
        c4 = c.T.reshape(HIGH, LOW, HIGH, LOW)
        s4 = s.T.reshape(HIGH, LOW, HIGH, LOW)
        full = np.zeros((HIGH, 2, LOW, ORBS, HIGH, 2, LOW, ORBS))
        for o in range(ORBS):
            full[:, 0, :, o, :, 0, :, o] = c4
            full[:, 1, :, o, :, 1, :, o] = c4
            full[:, 0, :, o, :, 1, :, o] = s4
            full[:, 1, :, o, :, 0, :, o] = -s4
        return full.reshape(HIGH * LANES, HIGH * LANES)

    spread = np.zeros((2, RING, 16, HIGH, 2, LOW, ORBS))
    for step in range(2):
        for y in range(G):
            spread[step, y // SLAB, step * SLAB + y % SLAB, y // LOW, :, y % LOW, :] = 1.0
    zero = np.zeros_like(both)
    made = [
        left([fc, fs], SLAB, 1),
        left([both], SLAB, 1),
        left([bc, bs], 4, 1),
        left([fc, fs], 1, 8),
        left([both], 1, 8),
        left([bc, bs], 1, 8),
        right(fc, fs),
        right(both, zero),
        right(bc, bs),
        spread.reshape(2, RING * 16, HIGH * LANES),
    ]
    return [m.astype(ml_dtypes.bfloat16) for m in made]


def swap_blocks(parts, lane):
    parts = list(parts)
    for bit in range(3):
        shift = 8 << bit
        low = ((lane >> (3 + bit)) & 1) == 0
        for i in range(8):
            if not (i >> bit) & 1:
                j = i | (1 << bit)
                a, b = parts[i], parts[j]
                parts[i] = jnp.where(low, a, pltpu.roll(b, shift, 1))
                parts[j] = jnp.where(low, pltpu.roll(a, LANES - shift, 1), b)
    return parts


def kernel(
    sources, walker_hbm, trial_hbm, field_hbm,
    fz_h, kz_h, bz_h, fx_h, kx_h, bx_h, fy_h, ky_h, by_h, spread_h,
    out_hbm, inter_ref,
    whole, trial, turned, own, near, pre_out, pre_in, sent, got, wa, wb, factor, back, late, field, field_near, field_out, field_in, field_all, field_t,
    asked, answer,
    fz, kz, bz, fx, kx, bx, fy, ky, by, spread, part, parts,
    load_sem, table_sem, near_send, near_recv, pre_send, pre_recv, in_send, in_recv, back_send, back_recv,
    fn_send, fn_recv, f_send, f_recv, ask_send, ask_recv, ring_send, ring_recv, sum_send, sum_recv, local_sem, out_sem,
):
    w = lax.axis_index("walk")
    me = lax.axis_index("grid")
    walks = lax.axis_size("walk")
    core = lax.rem(w, 2)
    parity = lax.rem(me + core, 2)
    distance = jnp.clip(sources[0] - w, -2, 2)
    turn = 1 - 2 * lax.rem(me // 2, 2)

    def ring(k):
        return lax.rem(me + k + 2 * RING, RING)

    ahead = (lax.rem(w + 2, walks), me)
    behind = (lax.rem(w - 2 + walks, walks), me)
    sibling = (w + 1 - 2 * core, me)
    def remote(src, dst, ssem, rsem, device):
        return pltpu.make_async_remote_copy(
            src_ref=src, dst_ref=dst, send_sem=ssem, recv_sem=rsem, device_id=device, device_id_type=MESH
        )

    load_w = pltpu.make_async_copy(walker_hbm.at[0], whole, load_sem.at[0])
    load_w.start()
    load_f = pltpu.make_async_copy(field_hbm, field, load_sem.at[1])
    load_f.start()
    barrier = pltpu.get_barrier_semaphore()
    for k in range(1, RING):
        pl.semaphore_signal(barrier, inc=1, device_id=(w, ring(k)), device_id_type=MESH)
    for device in (ahead, behind, sibling):
        pl.semaphore_signal(barrier, inc=1, device_id=device, device_id_type=MESH)

    lane = lax.broadcasted_iota(jnp.int32, (G, LANES), 1)
    sign = jnp.where(lax.broadcasted_iota(jnp.int32, (1, LANES), 1) < HALF, -1.0, 1.0).astype(F32)

    def flag(condition):
        return condition.astype(F32).astype(BF)

    to_sibling = 1 - 2 * core
    takes_own = flag(distance == 0)
    takes_near = flag(distance == to_sibling)
    takes_behind = flag(jnp.logical_or(distance == -2, distance == -to_sibling) & (distance < 0))
    takes_ahead = flag(jnp.logical_or(distance == 2, distance == -to_sibling) & (distance > 0))

    def target(group, j):
        step = jnp.where(parity == group, 2 * j + 2, 2 * j + 1)
        return lax.rem(me + turn * step + 2 * RING, RING)

    def near_copy(d, x):
        return remote(own.at[d, x], near.at[d, x], near_send, near_recv.at[d, x], sibling)

    def pre_copy(way, d, x):
        device = ahead if way == 0 else behind
        return remote(pre_out.at[way, d, x], pre_in.at[way, d, x], pre_send.at[way], pre_recv.at[way, d, x], device)

    load_w.wait()
    load_t = pltpu.make_async_copy(trial_hbm, trial, load_sem.at[2])
    table_loads = []
    pairs = ((fz_h, fz), (kz_h, kz), (bz_h, bz), (fx_h, fx), (kx_h, kx), (bx_h, bx), (fy_h, fy), (ky_h, ky), (by_h, by),
             (spread_h, spread))
    for i, (src, dst) in enumerate(pairs):
        c = pltpu.make_async_copy(src, dst, table_sem.at[i])
        table_loads.append(c)
    for c in [load_t] + table_loads:
        c.start()

    def shuffle(x, yh):
        rows = [whole[x, yh * LOW + i].astype(F32) for i in range(LOW)]
        moved = swap_blocks(rows, lane)
        for d in range(RING):
            own[d, x, yh] = moved[d].astype(BF)

    def shuffle_plane(x):
        def body(yh, _):
            shuffle(x, yh)
            return 0

        lax.fori_loop(0, HIGH, body, 0)

    def ask(way):
        device = behind if way == 0 else ahead
        return remote(asked, answer.at[way], ask_send.at[way], ask_recv.at[way], device)

    def near_field():
        return remote(field, field_near, fn_send, fn_recv, sibling)

    def field_copy(way):
        device = ahead if way == 0 else behind
        return remote(field_out.at[way], field_in.at[way], f_send.at[way], f_recv.at[way], device)

    asked[...] = jnp.full(asked.shape, distance.astype(F32), F32)
    load_f.wait()
    pl.semaphore_wait(barrier, RING - 1 + 3)
    near_field().start()
    for way in range(2):
        ask(way).start()

    def send_near(x, _):
        shuffle_plane(x)
        for j in range(4):
            for group in (1, 0):
                near_copy(target(group, j), x).start()
        return 0

    lax.fori_loop(0, SLAB, send_near, 0)

    for way in range(2):
        ask(way).wait_recv()
    wants = [flag(answer[0, 0, 0] == -1.0), flag(answer[1, 0, 0] == 1.0)]
    other = [flag(answer[0, 0, 0] != -1.0), flag(answer[1, 0, 0] != 1.0)]

    near_field().wait_recv()
    for way in range(2):
        field_out[way] = field[...] * other[way] + field_near[...] * wants[way]
        field_copy(way).start()

    def send_segment(s):
        group, x = s // SLAB, lax.rem(s, SLAB)
        for j in range(4):
            d = target(group, j)
            near_copy(d, x).wait_recv()
            for way in range(2):
                for yh in range(HIGH):
                    pre_out[way, d, x, yh] = own[d, x, yh] * other[way] + near[d, x, yh] * wants[way]
                pre_copy(way, d, x).start()

    def send_first(s, _):
        send_segment(s)
        return 0

    lax.fori_loop(0, SLAB, send_first, 0)

    def taken(mine, beside, from_behind, from_ahead):
        return mine * takes_own + beside * takes_near + from_behind * takes_behind + from_ahead * takes_ahead

    def in_copy(d, x):
        return remote(sent.at[d, x], got.at[me, x], in_send.at[d], in_recv.at[me], (w, d))

    def self_in(x):
        return pltpu.make_async_copy(sent.at[me, x], got.at[me, x], local_sem.at[x])

    def segment(s):
        group, x = s // SLAB, lax.rem(s, SLAB)
        for j in range(4):
            d = target(group, j)
            for way in range(2):
                pre_copy(way, d, x).wait_recv()
            for yh in range(HIGH):
                sent[d, x, yh] = taken(own[d, x, yh], near[d, x, yh], pre_in[0, d, x, yh], pre_in[1, d, x, yh])

            @pl.when(d != me)
            def _():
                in_copy(d, x).start()

            @pl.when(d == me)
            def _():
                self_in(x).start()

    def ring_field(d):
        return remote(field_all.at[me], field_all.at[me], ring_send.at[d], ring_recv.at[me], (w, d))

    def pick_field():
        for way in range(2):
            field_copy(way).wait_recv()
        field_all[me] = taken(field[...], field_near[...], field_in[0], field_in[1])
        for k in (4, 3, -3, 2, -2, 1, -1):
            ring_field(ring(k)).start()

    def last_fields():
        for k in range(1, RING):
            g = ring(k)
            remote(field_all.at[g], field_all.at[g], ring_send.at[g], ring_recv.at[g], (w, g)).wait_recv()

    def turn_trial():
        load_t.wait()

        def body(u, _):
            x, yh = u // HIGH, lax.rem(u, HIGH)
            old = trial[x, pl.ds(yh * LOW, LOW)].astype(F32).reshape(LOW * G, LANES)
            turned[u] = old.T.astype(BF)
            return 0

        lax.fori_loop(0, SLAB * HIGH, body, 0)

    def field_factors():
        for c in table_loads:
            c.wait()
        for i in range(RING):
            field_t[:, i * 16:(i + 1) * 16] = field_all[i].astype(F32).T

        def body(i, _):
            for step in range(2):
                rows = field_t[pl.ds(i * 400, 400), :].astype(BF)
                grown = jnp.exp(jnp.dot(rows, spread[step], preferred_element_type=F32))
                for yh in range(HIGH):
                    factor[step, pl.ds(i * 2, 2), :, yh] = cols(grown, yh).reshape(2, SLAB, G, LANES)
            return 0

        lax.fori_loop(0, 4, body, 0)

    def arrivals():
        for k in range(1, RING):
            g = ring(k)
            remote(sent.at[g], got.at[g], in_send.at[g], in_recv.at[g], (w, g)).wait_recv()
        for x in range(SLAB):
            self_in(x).wait()

    def cols(value, yh):
        return value[:, yh * LANES:(yh + 1) * LANES]

    def combined(value, yh, rows):
        c, s = cols(value, yh)[:rows], cols(value, yh)[rows:]
        return c + pltpu.roll(s, HALF, 1) * sign

    def stage_fz():
        arrivals()

        def body(g, _):
            data = [got[g, :, yh].astype(F32).reshape(200, LANES).astype(BF) for yh in range(HIGH)]
            value = jnp.dot(fz[...], jnp.concatenate(data, axis=1), preferred_element_type=F32)
            for yh in range(HIGH):
                wa[g, :, yh] = combined(value, yh, 200).reshape(SLAB, G, LANES)
            return 0

        lax.fori_loop(0, RING, body, 0)

    def stage_fy():
        def body(i, _):
            at = pl.ds(i * 2, 2)
            data = [wa[at, :, yh].reshape(400, LANES).astype(BF) for yh in range(HIGH)]
            value = jnp.dot(jnp.concatenate(data, axis=1), fy[...], preferred_element_type=F32)
            for yh in range(HIGH):
                wb[at, :, yh] = cols(value, yh).reshape(2, SLAB, G, LANES)
            return 0

        lax.fori_loop(0, 4, body, 0)

    def stage_fx():
        def body(i, _):
            at = pl.ds(pl.multiple_of(i * 8, 8), 8)
            data = [wb[:, :, yh, at].reshape(320, LANES).astype(BF) for yh in range(HIGH)]
            value = jnp.dot(fx[...], jnp.concatenate(data, axis=1), preferred_element_type=F32)
            lit = [
                (combined(value, yh, 320) * factor[0, :, :, yh, at].reshape(320, LANES)).astype(BF)
                for yh in range(HIGH)
            ]
            value = jnp.dot(kx[...], jnp.concatenate(lit, axis=1), preferred_element_type=F32)
            for yh in range(HIGH):
                wa[:, :, yh, at] = cols(value, yh).reshape(RING, SLAB, 8, LANES)
            return 0

        lax.fori_loop(0, 5, body, 0)

    def stage_kz():
        def body(g, _):
            data = [wa[g, :, yh].reshape(200, LANES).astype(BF) for yh in range(HIGH)]
            value = jnp.dot(kz[...], jnp.concatenate(data, axis=1), preferred_element_type=F32)
            for yh in range(HIGH):
                wb[g, :, yh] = cols(value, yh).reshape(SLAB, G, LANES)
            return 0

        lax.fori_loop(0, RING, body, 0)

    def stage_ky():
        def body(i, _):
            at = pl.ds(i * 2, 2)
            data = [wb[at, :, yh].reshape(400, LANES).astype(BF) for yh in range(HIGH)]
            value = jnp.dot(jnp.concatenate(data, axis=1), ky[...], preferred_element_type=F32)
            lit = [
                (cols(value, yh) * factor[1, at, :, yh].reshape(400, LANES)).astype(BF) for yh in range(HIGH)
            ]
            value = jnp.dot(jnp.concatenate(lit, axis=1), by[...], preferred_element_type=F32)
            for yh in range(HIGH):
                wa[at, :, yh] = cols(value, yh).reshape(2, SLAB, G, LANES)
            return 0

        lax.fori_loop(0, 4, body, 0)

    stages = (stage_fz, stage_fy, stage_fx, stage_kz, stage_ky)

    def slot(s, _):
        pl.when(s == 0)(pick_field)

        @pl.when(s < SLAB)
        def _():
            send_segment(s + SLAB)

        @pl.when(s < 2 * SLAB)
        def _():
            segment(s)

        pl.when(s == 2)(turn_trial)

        @pl.when(s == 4)
        def _():
            last_fields()
            field_factors()

        for k, stage in enumerate(stages):
            pl.when(s == SLAB + k + SLAB * parity)(stage)
        return 0

    lax.fori_loop(0, 3 * SLAB, slot, 0)

    def stage_bx(i, _):
        at = pl.ds(pl.multiple_of(i * 8, 8), 8)
        data = [wa[:, :, yh, at].reshape(320, LANES).astype(BF) for yh in range(HIGH)]
        value = jnp.dot(bx[...], jnp.concatenate(data, axis=1), preferred_element_type=F32)
        for yh in range(HIGH):
            wb[:, :, yh, at] = combined(value, yh, 320).reshape(RING, SLAB, 8, LANES)
        return 0

    lax.fori_loop(0, 5, stage_bx, 0)

    def back_copy(g, x):
        return remote(back.at[g, x], late.at[me, x], back_send.at[g], back_recv.at[me, x], (w, g))

    def self_back(x):
        return pltpu.make_async_copy(back.at[me, x], late.at[me, x], local_sem.at[x])

    def stage_bz(x, _):
        for h in range(2):
            data = [wb[h * 4:h * 4 + 4, x, yh].reshape(160, LANES).astype(BF) for yh in range(HIGH)]
            value = jnp.dot(bz[...], jnp.concatenate(data, axis=1), preferred_element_type=F32)
            for yh in range(HIGH):
                back[h * 4:h * 4 + 4, x, yh] = combined(value, yh, 160).reshape(4, G, LANES).astype(BF)
        for k in (4, 3, -3, 2, -2, 1, -1):
            back_copy(ring(k), x).start()
        self_back(x).start()
        return 0

    lax.fori_loop(0, SLAB, stage_bz, 0)

    part[...] = jnp.zeros_like(part)

    def store(x):
        return pltpu.make_async_copy(whole.at[x], out_hbm.at[0, x], out_sem.at[x])

    def finish(x, _):
        for k in range(1, RING):
            g = ring(k)
            remote(back.at[g, x], late.at[g, x], back_send.at[g], back_recv.at[g, x], (w, g)).wait_recv()
        self_back(x).wait()

        def body(yh, _):
            moved = swap_blocks([late[d, x, yh].astype(F32) for d in range(RING)], lane)
            for i in range(LOW):
                whole[x, yh * LOW + i] = moved[i].astype(BF)
            new = jnp.concatenate(moved, axis=0).astype(BF)
            part[...] += jnp.dot(turned[x * HIGH + yh], new, preferred_element_type=F32)
            return 0

        lax.fori_loop(0, HIGH, body, 0)
        store(x).start()
        return 0

    lax.fori_loop(0, SLAB, finish, 0)

    lower = part[HALF:, :]
    mine = part[:HALF, :] - pltpu.roll(lower, HALF, 1) * sign
    parts[me] = mine.astype(BF)

    def sum_copy(d):
        return remote(parts.at[me], parts.at[me], sum_send.at[d], sum_recv.at[me], (w, d))

    for k in (4, 3, -3, 2, -2, 1, -1):
        sum_copy(ring(k)).start()

    remote(own, near, near_send, near_recv.at[0, 0], sibling).wait_send()
    near_field().wait_send()
    for way in range(2):
        ask(way).wait_send()
        field_copy(way).wait_send()
        remote(pre_out.at[way], pre_in.at[way], pre_send.at[way], pre_recv.at[way, 0, 0], ahead).wait_send()
    for k in range(1, RING):
        d = ring(k)
        remote(sent.at[d], got.at[me], in_send.at[d], in_recv.at[me], (w, d)).wait_send()
        ring_field(d).wait_send()
        remote(back.at[d], late.at[me], back_send.at[d], back_recv.at[me, 0], (w, d)).wait_send()
    for x in range(SLAB):
        store(x).wait()

    for k in range(1, RING):
        g = ring(k)
        remote(parts.at[g], parts.at[g], sum_send.at[g], sum_recv.at[g], (w, g)).wait_recv()
    total = parts[0].astype(F32)
    for g in range(1, RING):
        total = total + parts[g].astype(F32)
    inter_ref[...] = total * (1.0 / math.sqrt(G**3))
    for k in range(1, RING):
        sum_copy(ring(k)).wait_send()


def on_device(walkers_in, trial, fields, sources):
    made = [jnp.asarray(t) for t in tables()]
    field = jnp.pad(fields.reshape(2 * SLAB, G * G), ((0, 16 - 2 * SLAB), (0, 0)))
    anywhere = pl.BlockSpec(memory_space=pl.ANY)
    chunk = (SLAB, HIGH, G, LANES)
    dma = pltpu.SemaphoreType.DMA
    scratch = [
        pltpu.VMEM((SLAB, G, G, LANES), BF),
        pltpu.VMEM((SLAB, G, G, LANES), BF),
        pltpu.VMEM((SLAB * HIGH, LANES, LOW * G), BF),
        pltpu.VMEM((RING,) + chunk, BF),
        pltpu.VMEM((RING,) + chunk, BF),
        pltpu.VMEM((2, RING) + chunk, BF),
        pltpu.VMEM((2, RING) + chunk, BF),
        pltpu.VMEM((RING,) + chunk, BF),
        pltpu.VMEM((RING,) + chunk, BF),
        pltpu.VMEM((RING,) + chunk, F32),
        pltpu.VMEM((RING,) + chunk, F32),
        pltpu.VMEM((2, RING) + chunk, F32),
        pltpu.VMEM((RING,) + chunk, BF),
        pltpu.VMEM((RING,) + chunk, BF),
        pltpu.VMEM((16, G * G), BF),
        pltpu.VMEM((16, G * G), BF),
        pltpu.VMEM((2, 16, G * G), BF),
        pltpu.VMEM((2, 16, G * G), BF),
        pltpu.VMEM((RING, 16, G * G), BF),
        pltpu.VMEM((G * G, RING * 16), F32),
        pltpu.VMEM((8, LANES), F32),
        pltpu.VMEM((2, 8, LANES), F32),
    ]
    scratch += [pltpu.VMEM(t.shape, BF) for t in made]
    scratch += [pltpu.VMEM((LANES, LANES), F32), pltpu.VMEM((RING, HALF, LANES), BF)]
    scratch += [
        dma((3,)), dma((len(made),)), dma, dma((RING, SLAB)), dma((2,)), dma((2, RING, SLAB)), dma((RING,)), dma((RING,)),
        dma((RING,)), dma((RING, SLAB)), dma, dma, dma((2,)), dma((2,)), dma((2,)), dma((2,)), dma((RING,)),
        dma((RING,)), dma((RING,)), dma((RING,)), dma((SLAB,)), dma((SLAB,)),
    ]
    walkers_out, inter = pl.pallas_call(
        kernel,
        out_shape=(
            jax.ShapeDtypeStruct((1, SLAB, G, G, LANES), BF),
            jax.ShapeDtypeStruct((HALF, LANES), F32),
        ),
        in_specs=[pl.BlockSpec(memory_space=pltpu.SMEM)] + [anywhere] * (3 + len(made)),
        out_specs=(anywhere, pl.BlockSpec(memory_space=pltpu.VMEM)),
        scratch_shapes=scratch,
        compiler_params=pltpu.CompilerParams(
            collective_id=0, has_side_effects=True, vmem_limit_bytes=62 * 2**20
        ),
        name="walkers",
    )(sources, walkers_in, trial, field, *made)
    return walkers_out, inter[None]


def solution(mesh):
    placed = (
        P("walk", "grid", None, None, None),
        P("grid", None, None, None),
        P(None, "walk", "grid", None),
        P("walk"),
    )
    return jax.shard_map(
        on_device,
        mesh=mesh,
        in_specs=placed,
        out_specs=(P("walk", "grid", None, None, None), P("walk", None, None)),
        check_vma=False,
    )
```

```python
import functools
import math

import jax
import jax.numpy as jnp
import ml_dtypes
import numpy as np
from jax import lax
from jax.experimental import pallas as pl
from jax.experimental.pallas import tpu as pltpu
from jax.sharding import PartitionSpec as P

MESH = pl.DeviceIdType.MESH
RATE = 0.001
G = 40
SLAB = 5
RING = 8
ORBS = 8
LOW = 8
HIGH = 5
LANES = 128
HALF = 64
BF = jnp.bfloat16
F32 = jnp.float32


def tables():
    n = np.arange(G)
    angle = (n[:, None] * n[None, :] % G) * (2.0 * math.pi / G)
    cos = (np.cos(angle) / math.sqrt(G)).astype(ml_dtypes.bfloat16).astype(np.float64)
    sin = (np.sin(angle) / math.sqrt(G)).astype(ml_dtypes.bfloat16).astype(np.float64)
    signed = np.where(n < G // 2, n, n - G)
    damp = np.exp(-0.5 * RATE * signed**2)
    fc, fs = cos.T * damp[None, :], sin.T * damp[None, :]
    bc, bs = damp[:, None] * cos.T, -damp[:, None] * sin.T
    both = (cos * damp[None, :] ** 2) @ cos.T + (sin * damp[None, :] ** 2) @ sin.T

    def left(parts, before, after):
        grown = [np.kron(np.kron(np.eye(before), p), np.eye(after)) for p in parts]
        return np.concatenate(grown, axis=0)

    def right(c, s):
        c4 = c.T.reshape(HIGH, LOW, HIGH, LOW)
        s4 = s.T.reshape(HIGH, LOW, HIGH, LOW)
        full = np.zeros((HIGH, 2, LOW, ORBS, HIGH, 2, LOW, ORBS))
        for o in range(ORBS):
            full[:, 0, :, o, :, 0, :, o] = c4
            full[:, 1, :, o, :, 1, :, o] = c4
            full[:, 0, :, o, :, 1, :, o] = s4
            full[:, 1, :, o, :, 0, :, o] = -s4
        return full.reshape(HIGH * LANES, HIGH * LANES)

    spread = np.zeros((2, RING, 16, HIGH, 2, LOW, ORBS))
    for step in range(2):
        for y in range(G):
            spread[step, y // SLAB, y % SLAB * 2 + step, y // LOW, :, y % LOW, :] = 1.0
    zero = np.zeros_like(both)
    made = [
        left([fc, fs], SLAB, 1),
        left([both], SLAB, 1),
        left([bc, bs], 4, 1),
        left([fc, fs], 1, 8),
        left([both], 1, 8),
        left([bc, bs], 1, 8),
        right(fc, fs),
        right(both, zero),
        right(bc, bs),
        spread.reshape(2, RING * 16, HIGH * LANES),
    ]
    return [m.astype(ml_dtypes.bfloat16) for m in made]


def swap_blocks(parts, lane):
    parts = list(parts)
    for bit in range(3):
        shift = 8 << bit
        low = ((lane >> (3 + bit)) & 1) == 0
        for i in range(8):
            if not (i >> bit) & 1:
                j = i | (1 << bit)
                a, b = parts[i], parts[j]
                parts[i] = jnp.where(low, a, pltpu.roll(b, shift, 1))
                parts[j] = jnp.where(low, pltpu.roll(a, LANES - shift, 1), b)
    return parts


def kernel(
    sources, walker_hbm, trial_hbm, field_hbm,
    fz_h, kz_h, bz_h, fx_h, kx_h, bx_h, fy_h, ky_h, by_h, spread_h,
    out_hbm, inter_ref,
    whole, trial, turned, own, near, pre_out, pre_in, sent, got, wa, wb, factor, back, late, raw, field, field_near, field_out, field_in, field_all, field_t,
    asked, answer,
    fz, kz, bz, fx, kx, bx, fy, ky, by, spread, part, parts,
    load_sem, plane_sem, table_sem, near_send, near_recv, pre_send, pre_recv, in_send, in_recv, back_send, back_recv,
    fn_send, fn_recv, f_send, f_recv, ask_send, ask_recv, ring_send, ring_recv, sum_send, sum_recv, local_sem, out_sem,
):
    w = lax.axis_index("walk")
    me = lax.axis_index("grid")
    walks = lax.axis_size("walk")
    core = lax.rem(w, 2)
    parity = lax.rem(me + core, 2)
    distance = jnp.clip(sources[0] - w, -2, 2)
    turn = 1 - 2 * core

    def ring(k):
        return lax.rem(me + k + 2 * RING, RING)

    ahead = (lax.rem(w + 2, walks), me)
    behind = (lax.rem(w - 2 + walks, walks), me)
    sibling = (w + 1 - 2 * core, me)
    def remote(src, dst, ssem, rsem, device):
        return pltpu.make_async_remote_copy(
            src_ref=src, dst_ref=dst, send_sem=ssem, recv_sem=rsem, device_id=device, device_id_type=MESH
        )

    barrier = pltpu.get_barrier_semaphore()
    for k in range(1, RING):
        pl.semaphore_signal(barrier, inc=1, device_id=(w, ring(k)), device_id_type=MESH)
    for device in (ahead, behind, sibling):
        pl.semaphore_signal(barrier, inc=1, device_id=device, device_id_type=MESH)

    load_f = pltpu.make_async_copy(field_hbm, raw, load_sem.at[1])
    load_f.start()
    load_w = [pltpu.make_async_copy(walker_hbm.at[0, x], whole.at[x], plane_sem.at[x]) for x in range(SLAB)]
    for c in load_w:
        c.start()

    lane = lax.broadcasted_iota(jnp.int32, (G, LANES), 1)
    sign = jnp.where(lax.broadcasted_iota(jnp.int32, (1, LANES), 1) < HALF, -1.0, 1.0).astype(F32)

    def flag(condition):
        return condition.astype(F32).astype(BF)

    to_sibling = 1 - 2 * core
    takes_own = flag(distance == 0)
    takes_near = flag(distance == to_sibling)
    takes_behind = flag(jnp.logical_or(distance == -2, distance == -to_sibling) & (distance < 0))
    takes_ahead = flag(jnp.logical_or(distance == 2, distance == -to_sibling) & (distance > 0))

    def target(group, j):
        step = jnp.where(parity == group, 2 * j + 2, 2 * j + 1)
        return lax.rem(me + turn * step + 2 * RING, RING)

    def near_copy(d, x):
        return remote(own.at[d, x], near.at[d, x], near_send, near_recv.at[d, x], sibling)

    def pre_copy(way, d, x):
        device = ahead if way == 0 else behind
        return remote(pre_out.at[way, d, x], pre_in.at[way, d, x], pre_send.at[way], pre_recv.at[way, d, x], device)

    def shuffle(x, yh):
        rows = [whole[x, yh * LOW + i] for i in range(LOW)]
        moved = swap_blocks(rows, lane)
        for d in range(RING):
            own[d, x, yh] = moved[d]

    def shuffle_plane(x):
        def body(yh, _):
            shuffle(x, yh)
            return 0

        lax.fori_loop(0, HIGH, body, 0)

    def ask(way):
        device = behind if way == 0 else ahead
        return remote(asked, answer.at[way], ask_send.at[way], ask_recv.at[way], device)

    def near_field():
        return remote(field, field_near, fn_send, fn_recv, sibling)

    def field_copy(way):
        device = ahead if way == 0 else behind
        return remote(field_out.at[way], field_in.at[way], f_send.at[way], f_recv.at[way], device)

    asked[...] = jnp.full(asked.shape, distance.astype(F32), F32)
    load_f.wait()
    rows = [raw[y].astype(F32) for y in range(SLAB)] + [jnp.zeros((6, G * G), F32)]
    field[...] = jnp.concatenate(rows, axis=0).astype(BF)
    load_w[0].wait()
    shuffle_plane(0)
    pl.semaphore_wait(barrier, RING - 1 + 3)
    near_field().start()
    for way in range(2):
        ask(way).start()

    def send_near(x):
        for j in range(4):
            for group in (1, 0):
                near_copy(target(group, j), x).start()

    def send_segment(s):
        group, x = s // SLAB, lax.rem(s, SLAB)
        for j in range(4):
            d = target(group, j)
            near_copy(d, x).wait_recv()
            for way in range(2):
                for yh in range(HIGH):
                    pre_out[way, d, x, yh] = own[d, x, yh] * other[way] + near[d, x, yh] * wants[way]
                pre_copy(way, d, x).start()

    send_near(0)
    load_t = pltpu.make_async_copy(trial_hbm, trial, load_sem.at[2])
    table_loads = []
    pairs = ((fz_h, fz), (kz_h, kz), (bz_h, bz), (fx_h, fx), (kx_h, kx), (bx_h, bx), (fy_h, fy), (ky_h, ky), (by_h, by),
             (spread_h, spread))
    for i, (src, dst) in enumerate(pairs):
        c = pltpu.make_async_copy(src, dst, table_sem.at[i])
        table_loads.append(c)
    for way in range(2):
        ask(way).wait_recv()
    wants = [flag(answer[0, 0, 0] == -1.0), flag(answer[1, 0, 0] == 1.0)]
    other = [flag(answer[0, 0, 0] != -1.0), flag(answer[1, 0, 0] != 1.0)]

    near_field().wait_recv()
    for way in range(2):
        field_out[way] = field[...] * other[way] + field_near[...] * wants[way]
        field_copy(way).start()
    send_segment(0)

    for c in load_w[1:]:
        c.wait()
    for c in [load_t] + table_loads:
        c.start()

    def send_many(s, _):
        send_segment(s)
        return 0

    def taken(mine, beside, from_behind, from_ahead):
        return mine * takes_own + beside * takes_near + from_behind * takes_behind + from_ahead * takes_ahead

    def in_copy(d, x):
        return remote(sent.at[d, x], got.at[me, x], in_send.at[d], in_recv.at[me], (w, d))

    def self_in(x):
        return pltpu.make_async_copy(sent.at[me, x], got.at[me, x], local_sem.at[x])

    def segment(s):
        group, x = s // SLAB, lax.rem(s, SLAB)
        for j in range(4):
            d = target(group, j)
            for way in range(2):
                pre_copy(way, d, x).wait_recv()
            for yh in range(HIGH):
                sent[d, x, yh] = taken(own[d, x, yh], near[d, x, yh], pre_in[0, d, x, yh], pre_in[1, d, x, yh])

            @pl.when(d != me)
            def _():
                in_copy(d, x).start()

            @pl.when(d == me)
            def _():
                self_in(x).start()

    def ring_field(k, origin=0):
        g = ring(origin)
        n = k + 2 if origin == 0 else k + 6
        return remote(field_all.at[g], field_all.at[g], ring_send.at[n], ring_recv.at[g], (w, ring(k)))

    def field_from(origin):
        g = ring(origin)
        remote(field_all.at[g], field_all.at[g], ring_send.at[0], ring_recv.at[g], (w, ring(1))).wait_recv()

    field_sends = ((1, 0), (-1, 0), (2, 0), (-2, 0), (1, -2), (2, -2), (-1, 2))

    def pick_field():
        for way in range(2):
            field_copy(way).wait_recv()
        field_all[me] = taken(field[...], field_near[...], field_in[0], field_in[1])
        for k, origin in field_sends[:4]:
            ring_field(k, origin).start()

    def pass_field():
        field_from(-2)
        field_from(2)
        for k, origin in field_sends[4:]:
            ring_field(k, origin).start()

    def last_fields():
        for origin in (-1, 1, -3, 3, 4):
            field_from(origin)

    def turn_trial():
        load_t.wait()

        def body(u, _):
            x, yh = u // HIGH, lax.rem(u, HIGH)
            old = trial[x, pl.ds(yh * LOW, LOW)].astype(F32).reshape(LOW * G, LANES)
            turned[u] = old.T.astype(BF)
            return 0

        lax.fori_loop(0, SLAB * HIGH, body, 0)

    def field_factors():
        for c in table_loads:
            c.wait()
        for i in range(RING):
            field_t[:, i * 16:(i + 1) * 16] = field_all[i].astype(F32).T

        def body(i, _):
            for step in range(2):
                rows = field_t[pl.ds(i * 400, 400), :].astype(BF)
                grown = jnp.exp(jnp.dot(rows, spread[step], preferred_element_type=F32))
                for yh in range(HIGH):
                    factor[step, pl.ds(i * 2, 2), :, yh] = cols(grown, yh).reshape(2, SLAB, G, LANES)
            return 0

        lax.fori_loop(0, 4, body, 0)

    def arrivals():
        for k in range(1, RING):
            g = ring(k)
            remote(sent.at[g], got.at[g], in_send.at[g], in_recv.at[g], (w, g)).wait_recv()
        for x in range(SLAB):
            self_in(x).wait()

    def cols(value, yh):
        return value[:, yh * LANES:(yh + 1) * LANES]

    def combined(value, yh, rows):
        c, s = cols(value, yh)[:rows], cols(value, yh)[rows:]
        return c + pltpu.roll(s, HALF, 1) * sign

    def stage_fz():
        arrivals()

        def body(g, _):
            data = [got[g, :, yh].astype(F32).reshape(200, LANES).astype(BF) for yh in range(HIGH)]
            value = jnp.dot(fz[...], jnp.concatenate(data, axis=1), preferred_element_type=F32)
            for yh in range(HIGH):
                wa[g, :, yh] = combined(value, yh, 200).reshape(SLAB, G, LANES)
            return 0

        lax.fori_loop(0, RING, body, 0)

    def stage_fy():
        def body(i, _):
            at = pl.ds(i * 2, 2)
            data = [wa[at, :, yh].reshape(400, LANES).astype(BF) for yh in range(HIGH)]
            value = jnp.dot(jnp.concatenate(data, axis=1), fy[...], preferred_element_type=F32)
            for yh in range(HIGH):
                wb[at, :, yh] = cols(value, yh).reshape(2, SLAB, G, LANES)
            return 0

        lax.fori_loop(0, 4, body, 0)

    def stage_fx():
        def body(i, _):
            at = pl.ds(pl.multiple_of(i * 8, 8), 8)
            data = [wb[:, :, yh, at].reshape(320, LANES).astype(BF) for yh in range(HIGH)]
            value = jnp.dot(fx[...], jnp.concatenate(data, axis=1), preferred_element_type=F32)
            lit = [
                (combined(value, yh, 320) * factor[0, :, :, yh, at].reshape(320, LANES)).astype(BF)
                for yh in range(HIGH)
            ]
            value = jnp.dot(kx[...], jnp.concatenate(lit, axis=1), preferred_element_type=F32)
            for yh in range(HIGH):
                wa[:, :, yh, at] = cols(value, yh).reshape(RING, SLAB, 8, LANES)
            return 0

        lax.fori_loop(0, 5, body, 0)

    def stage_kz():
        def body(g, _):
            data = [wa[g, :, yh].reshape(200, LANES).astype(BF) for yh in range(HIGH)]
            value = jnp.dot(kz[...], jnp.concatenate(data, axis=1), preferred_element_type=F32)
            for yh in range(HIGH):
                wb[g, :, yh] = cols(value, yh).reshape(SLAB, G, LANES)
            return 0

        lax.fori_loop(0, RING, body, 0)

    def stage_ky():
        def body(i, _):
            at = pl.ds(i * 2, 2)
            data = [wb[at, :, yh].reshape(400, LANES).astype(BF) for yh in range(HIGH)]
            value = jnp.dot(jnp.concatenate(data, axis=1), ky[...], preferred_element_type=F32)
            lit = [
                (cols(value, yh) * factor[1, at, :, yh].reshape(400, LANES)).astype(BF) for yh in range(HIGH)
            ]
            value = jnp.dot(jnp.concatenate(lit, axis=1), by[...], preferred_element_type=F32)
            for yh in range(HIGH):
                wa[at, :, yh] = cols(value, yh).reshape(2, SLAB, G, LANES)
            return 0

        lax.fori_loop(0, 4, body, 0)

    stages = (stage_fz, stage_fy, stage_fx, stage_kz, stage_ky)

    def slot(s, _):
        @pl.when(s < SLAB - 1)
        def _():
            shuffle_plane(s + 1)
            send_near(s + 1)
            send_segment(s + 1)

        pl.when(s == 0)(pick_field)

        @pl.when(jnp.logical_or(s == 3, s == 4))
        def _():
            lax.fori_loop(2 * s - 1, 3 * s - 2, send_many, 0)

        @pl.when(s < 2 * SLAB)
        def _():
            segment(s)

        pl.when(s == 2)(pass_field)

        @pl.when(s == 4)
        def _():
            last_fields()
            field_factors()

        for k, stage in enumerate(stages):
            pl.when(s == SLAB + k + SLAB * parity)(stage)
        return 0

    lax.fori_loop(0, 3 * SLAB, slot, 0)

    def stage_bx(i, _):
        at = pl.ds(pl.multiple_of(i * 8, 8), 8)
        data = [wa[:, :, yh, at].reshape(320, LANES).astype(BF) for yh in range(HIGH)]
        value = jnp.dot(bx[...], jnp.concatenate(data, axis=1), preferred_element_type=F32)
        for yh in range(HIGH):
            wb[:, :, yh, at] = combined(value, yh, 320).reshape(RING, SLAB, 8, LANES)
        return 0

    lax.fori_loop(0, 5, stage_bx, 0)

    def back_copy(g, x):
        return remote(back.at[g, x], late.at[me, x], back_send.at[g], back_recv.at[me, x], (w, g))

    def self_back(x):
        return pltpu.make_async_copy(back.at[me, x], late.at[me, x], local_sem.at[x])

    def stage_bz(x, _):
        for h in range(2):
            data = [wb[h * 4:h * 4 + 4, x, yh].reshape(160, LANES).astype(BF) for yh in range(HIGH)]
            value = jnp.dot(bz[...], jnp.concatenate(data, axis=1), preferred_element_type=F32)
            for yh in range(HIGH):
                back[h * 4:h * 4 + 4, x, yh] = combined(value, yh, 160).reshape(4, G, LANES).astype(BF)
        for k in (4, 3, -3, 2, -2, 1, -1):
            back_copy(ring(k), x).start()
        self_back(x).start()
        return 0

    lax.fori_loop(0, SLAB, stage_bz, 0)

    turn_trial()

    part[...] = jnp.zeros_like(part)

    def store(x):
        return pltpu.make_async_copy(whole.at[x], out_hbm.at[0, x], out_sem.at[x])

    def finish(x, _):
        for k in range(1, RING):
            g = ring(k)
            remote(back.at[g, x], late.at[g, x], back_send.at[g], back_recv.at[g, x], (w, g)).wait_recv()
        self_back(x).wait()

        def body(yh, _):
            moved = swap_blocks([late[d, x, yh] for d in range(RING)], lane)
            for i in range(LOW):
                whole[x, yh * LOW + i] = moved[i]
            new = jnp.concatenate([m.astype(F32) for m in moved], axis=0).astype(BF)
            part[...] += jnp.dot(turned[x * HIGH + yh], new, preferred_element_type=F32)
            return 0

        lax.fori_loop(0, HIGH, body, 0)
        store(x).start()
        return 0

    lax.fori_loop(0, SLAB, finish, 0)

    lower = part[HALF:, :]
    mine = part[:HALF, :] - pltpu.roll(lower, HALF, 1) * sign
    parts[me] = mine.astype(BF)

    def sum_copy(d):
        return remote(parts.at[me], parts.at[me], sum_send.at[d], sum_recv.at[me], (w, d))

    for k in (4, 3, -3, 2, -2, 1, -1):
        sum_copy(ring(k)).start()

    remote(own, near, near_send, near_recv.at[0, 0], sibling).wait_send()
    near_field().wait_send()
    for k, origin in field_sends:
        ring_field(k, origin).wait_send()
    for way in range(2):
        ask(way).wait_send()
        field_copy(way).wait_send()
        remote(pre_out.at[way], pre_in.at[way], pre_send.at[way], pre_recv.at[way, 0, 0], ahead).wait_send()
    for k in range(1, RING):
        d = ring(k)
        remote(sent.at[d], got.at[me], in_send.at[d], in_recv.at[me], (w, d)).wait_send()
        remote(back.at[d], late.at[me], back_send.at[d], back_recv.at[me, 0], (w, d)).wait_send()
    for x in range(SLAB):
        store(x).wait()

    for k in range(1, RING):
        g = ring(k)
        remote(parts.at[g], parts.at[g], sum_send.at[g], sum_recv.at[g], (w, g)).wait_recv()
    total = parts[0].astype(F32)
    for g in range(1, RING):
        total = total + parts[g].astype(F32)
    inter_ref[...] = total * (1.0 / math.sqrt(G**3))
    for k in range(1, RING):
        sum_copy(ring(k)).wait_send()


def hand_over(walkers, inter, walkers_out, inter_out, held, held_inter, in_sem, out_sem):
    steps = [(walkers.at[0, x], held.at[x], walkers_out.at[0, x]) for x in range(SLAB)]
    steps.append((inter, held_inter, inter_out.at[0]))
    inward = [pltpu.make_async_copy(a, b, in_sem.at[i]) for i, (a, b, _) in enumerate(steps)]
    outward = [pltpu.make_async_copy(b, c, out_sem.at[i]) for i, (_, b, c) in enumerate(steps)]
    for c in inward:
        c.start()
    for i, c in enumerate(outward):
        inward[i].wait()
        c.start()
    for c in outward:
        c.wait()


def on_device(walkers_in, trial, fields, sources):
    made = [jnp.asarray(t) for t in tables()]
    anywhere = pl.BlockSpec(memory_space=pl.ANY)
    chunk = (SLAB, HIGH, G, LANES)
    dma = pltpu.SemaphoreType.DMA
    scratch = [
        pltpu.VMEM((SLAB, G, G, LANES), BF),
        pltpu.VMEM((SLAB, G, G, LANES), BF),
        pltpu.VMEM((SLAB * HIGH, LANES, LOW * G), BF),
        pltpu.VMEM((RING,) + chunk, BF),
        pltpu.VMEM((RING,) + chunk, BF),
        pltpu.VMEM((2, RING) + chunk, BF),
        pltpu.VMEM((2, RING) + chunk, BF),
        pltpu.VMEM((RING,) + chunk, BF),
        pltpu.VMEM((RING,) + chunk, BF),
        pltpu.VMEM((RING,) + chunk, F32),
        pltpu.VMEM((RING,) + chunk, F32),
        pltpu.VMEM((2, RING) + chunk, F32),
        pltpu.VMEM((RING,) + chunk, BF),
        pltpu.VMEM((RING,) + chunk, BF),
        pltpu.VMEM((SLAB, 2, G * G), BF),
        pltpu.VMEM((16, G * G), BF),
        pltpu.VMEM((16, G * G), BF),
        pltpu.VMEM((2, 16, G * G), BF),
        pltpu.VMEM((2, 16, G * G), BF),
        pltpu.VMEM((RING, 16, G * G), BF),
        pltpu.VMEM((G * G, RING * 16), F32),
        pltpu.VMEM((8, LANES), F32),
        pltpu.VMEM((2, 8, LANES), F32),
    ]
    scratch += [pltpu.VMEM(t.shape, BF) for t in made]
    scratch += [pltpu.VMEM((LANES, LANES), F32), pltpu.VMEM((RING, HALF, LANES), BF)]
    scratch += [
        dma((3,)), dma((SLAB,)), dma((len(made),)), dma, dma((RING, SLAB)), dma((2,)), dma((2, RING, SLAB)), dma((RING,)), dma((RING,)),
        dma((RING,)), dma((RING, SLAB)), dma, dma, dma((2,)), dma((2,)), dma((2,)), dma((2,)), dma((9,)),
        dma((RING,)), dma((RING,)), dma((RING,)), dma((SLAB,)), dma((SLAB,)),
    ]
    walkers_out, inter = pl.pallas_call(
        kernel,
        out_shape=(
            jax.ShapeDtypeStruct((1, SLAB, G, G, LANES), BF),
            jax.ShapeDtypeStruct((HALF, LANES), F32),
        ),
        in_specs=[pl.BlockSpec(memory_space=pltpu.SMEM)] + [anywhere] * (3 + len(made)),
        out_specs=(anywhere, pl.BlockSpec(memory_space=pltpu.VMEM)),
        scratch_shapes=scratch,
        compiler_params=pltpu.CompilerParams(
            collective_id=0, has_side_effects=True, vmem_limit_bytes=62 * 2**20
        ),
        name="walkers",
    )(sources, walkers_in, trial, fields.reshape(2, SLAB, G * G).transpose(1, 0, 2), *made)
    return pl.pallas_call(
        hand_over,
        out_shape=(
            jax.ShapeDtypeStruct((1, SLAB, G, G, LANES), BF),
            jax.ShapeDtypeStruct((1, HALF, LANES), F32),
        ),
        in_specs=[anywhere] * 2,
        out_specs=(anywhere,) * 2,
        scratch_shapes=[
            pltpu.VMEM((SLAB, G, G, LANES), BF),
            pltpu.VMEM((HALF, LANES), F32),
            dma((SLAB + 1,)),
            dma((SLAB + 1,)),
        ],
        name="results",
    )(walkers_out, inter)


def solution(mesh):
    placed = (
        P("walk", "grid", None, None, None),
        P("grid", None, None, None),
        P(None, "walk", "grid", None),
        P("walk"),
    )
    return jax.shard_map(
        on_device,
        mesh=mesh,
        in_specs=placed,
        out_specs=(P("walk", "grid", None, None, None), P("walk", None, None)),
        check_vma=False,
    )
```

```python
import functools
import math

import jax
import jax.numpy as jnp
import ml_dtypes
import numpy as np
from jax import lax
from jax.experimental import pallas as pl
from jax.experimental.pallas import tpu as pltpu
from jax.sharding import PartitionSpec as P

MESH = pl.DeviceIdType.MESH
RATE = 0.001
G = 40
SLAB = 5
RING = 8
ORBS = 8
LOW = 8
HIGH = 5
LANES = 128
HALF = 64
BF = jnp.bfloat16
F32 = jnp.float32


def tables():
    n = np.arange(G)
    angle = (n[:, None] * n[None, :] % G) * (2.0 * math.pi / G)
    cos = (np.cos(angle) / math.sqrt(G)).astype(ml_dtypes.bfloat16).astype(np.float64)
    sin = (np.sin(angle) / math.sqrt(G)).astype(ml_dtypes.bfloat16).astype(np.float64)
    signed = np.where(n < G // 2, n, n - G)
    damp = np.exp(-0.5 * RATE * signed**2)
    fc, fs = cos.T * damp[None, :], sin.T * damp[None, :]
    bc, bs = damp[:, None] * cos.T, -damp[:, None] * sin.T
    both = (cos * damp[None, :] ** 2) @ cos.T + (sin * damp[None, :] ** 2) @ sin.T

    def left(parts, before, after):
        grown = [np.kron(np.kron(np.eye(before), p), np.eye(after)) for p in parts]
        return np.concatenate(grown, axis=0)

    def right(c, s):
        c4 = c.T.reshape(HIGH, LOW, HIGH, LOW)
        s4 = s.T.reshape(HIGH, LOW, HIGH, LOW)
        full = np.zeros((HIGH, 2, LOW, ORBS, HIGH, 2, LOW, ORBS))
        for o in range(ORBS):
            full[:, 0, :, o, :, 0, :, o] = c4
            full[:, 1, :, o, :, 1, :, o] = c4
            full[:, 0, :, o, :, 1, :, o] = s4
            full[:, 1, :, o, :, 0, :, o] = -s4
        return full.reshape(HIGH * LANES, HIGH * LANES)

    spread = np.zeros((2, RING, 16, HIGH, 2, LOW, ORBS))
    for step in range(2):
        for y in range(G):
            spread[step, y // SLAB, y % SLAB * 2 + step, y // LOW, :, y % LOW, :] = 1.0
    zero = np.zeros_like(both)
    made = [
        left([fc, fs], 4, 1),
        left([both], SLAB, 1),
        left([bc, bs], 4, 1),
        left([fc, fs], 1, 8),
        left([both], 1, 8),
        left([bc, bs], 1, 8),
        right(fc, fs),
        right(both, zero),
        right(bc, bs),
        spread.reshape(2, RING * 16, HIGH * LANES),
    ]
    return [m.astype(ml_dtypes.bfloat16) for m in made]


def swap_blocks(parts, lane):
    parts = list(parts)
    for bit in range(3):
        shift = 8 << bit
        low = ((lane >> (3 + bit)) & 1) == 0
        for i in range(8):
            if not (i >> bit) & 1:
                j = i | (1 << bit)
                a, b = parts[i], parts[j]
                parts[i] = jnp.where(low, a, pltpu.roll(b, shift, 1))
                parts[j] = jnp.where(low, pltpu.roll(a, LANES - shift, 1), b)
    return parts


def kernel(
    sources, walker_hbm, trial_hbm, field_hbm,
    fz_h, kz_h, bz_h, fx_h, kx_h, bx_h, fy_h, ky_h, by_h, spread_h,
    out_hbm, inter_ref,
    whole, trial, turned, own, near, pre_out, pre_in, sent, got, wa, wb, factor, back, late, raw, field, field_near, field_out, field_in, field_all, field_t,
    asked, answer,
    fz, kz, bz, fx, kx, bx, fy, ky, by, spread, part, parts,
    load_sem, plane_sem, table_sem, near_send, near_recv, pre_send, pre_recv, in_send, in_recv, back_send, back_recv,
    fn_send, fn_recv, f_send, f_recv, ask_send, ask_recv, ring_send, ring_recv, sum_send, sum_recv, local_sem, out_sem,
):
    w = lax.axis_index("walk")
    me = lax.axis_index("grid")
    walks = lax.axis_size("walk")
    core = lax.rem(w, 2)
    parity = lax.rem(me + core, 2)
    distance = jnp.clip(sources[0] - w, -2, 2)
    turn = 1 - 2 * core

    def ring(k):
        return lax.rem(me + k + 2 * RING, RING)

    ahead = (lax.rem(w + 2, walks), me)
    behind = (lax.rem(w - 2 + walks, walks), me)
    sibling = (w + 1 - 2 * core, me)
    def remote(src, dst, ssem, rsem, device):
        return pltpu.make_async_remote_copy(
            src_ref=src, dst_ref=dst, send_sem=ssem, recv_sem=rsem, device_id=device, device_id_type=MESH
        )

    barrier = pltpu.get_barrier_semaphore()
    for k in range(1, RING):
        pl.semaphore_signal(barrier, inc=1, device_id=(w, ring(k)), device_id_type=MESH)
    for device in (ahead, behind, sibling):
        pl.semaphore_signal(barrier, inc=1, device_id=device, device_id_type=MESH)

    load_f = pltpu.make_async_copy(field_hbm, raw, load_sem.at[1])
    load_f.start()
    load_w = [pltpu.make_async_copy(walker_hbm.at[0, x], whole.at[x], plane_sem.at[x]) for x in range(SLAB)]
    for c in load_w:
        c.start()

    lane = lax.broadcasted_iota(jnp.int32, (G, LANES), 1)
    sign = jnp.where(lax.broadcasted_iota(jnp.int32, (1, LANES), 1) < HALF, -1.0, 1.0).astype(F32)

    def flag(condition):
        return condition.astype(F32).astype(BF)

    to_sibling = 1 - 2 * core
    takes_own = flag(distance == 0)
    takes_near = flag(distance == to_sibling)
    takes_behind = flag(jnp.logical_or(distance == -2, distance == -to_sibling) & (distance < 0))
    takes_ahead = flag(jnp.logical_or(distance == 2, distance == -to_sibling) & (distance > 0))

    def target(group, j):
        step = jnp.where(parity == group, 2 * j + 2, 2 * j + 1)
        return lax.rem(me + turn * step + 2 * RING, RING)

    def near_copy(d, x):
        return remote(own.at[d, x], near.at[d, x], near_send, near_recv.at[d, x], sibling)

    def pre_copy(way, d, x):
        device = ahead if way == 0 else behind
        return remote(pre_out.at[way, d, x], pre_in.at[way, d, x], pre_send.at[way], pre_recv.at[way, d, x], device)

    def shuffle(x, yh):
        rows = [whole[x, yh * LOW + i] for i in range(LOW)]
        moved = swap_blocks(rows, lane)
        for d in range(RING):
            own[d, x, yh] = moved[d]

    def shuffle_plane(x):
        def body(yh, _):
            shuffle(x, yh)
            return 0

        lax.fori_loop(0, HIGH, body, 0)

    def ask(way):
        device = behind if way == 0 else ahead
        return remote(asked, answer.at[way], ask_send.at[way], ask_recv.at[way], device)

    def near_field():
        return remote(field, field_near, fn_send, fn_recv, sibling)

    def field_copy(way):
        device = ahead if way == 0 else behind
        return remote(field_out.at[way], field_in.at[way], f_send.at[way], f_recv.at[way], device)

    asked[...] = jnp.full(asked.shape, distance.astype(F32), F32)
    load_f.wait()
    rows = [raw[y].astype(F32) for y in range(SLAB)] + [jnp.zeros((6, G * G), F32)]
    field[...] = jnp.concatenate(rows, axis=0).astype(BF)
    load_w[0].wait()
    shuffle_plane(0)
    pl.semaphore_wait(barrier, RING - 1 + 3)
    near_field().start()
    for way in range(2):
        ask(way).start()

    def send_near(x):
        for j in range(4):
            for group in (1, 0):
                near_copy(target(group, j), x).start()

    def send_segment(s):
        group, x = s // SLAB, lax.rem(s, SLAB)
        for j in range(4):
            d = target(group, j)
            near_copy(d, x).wait_recv()
            for way in range(2):
                for yh in range(HIGH):
                    pre_out[way, d, x, yh] = own[d, x, yh] * other[way] + near[d, x, yh] * wants[way]
                pre_copy(way, d, x).start()

    send_near(0)
    load_t = pltpu.make_async_copy(trial_hbm, trial, load_sem.at[2])
    table_loads = []
    pairs = ((fz_h, fz), (kz_h, kz), (bz_h, bz), (fx_h, fx), (kx_h, kx), (bx_h, bx), (fy_h, fy), (ky_h, ky), (by_h, by),
             (spread_h, spread))
    for i, (src, dst) in enumerate(pairs):
        c = pltpu.make_async_copy(src, dst, table_sem.at[i])
        table_loads.append(c)
    for way in range(2):
        ask(way).wait_recv()
    wants = [flag(answer[0, 0, 0] == -1.0), flag(answer[1, 0, 0] == 1.0)]
    other = [flag(answer[0, 0, 0] != -1.0), flag(answer[1, 0, 0] != 1.0)]

    near_field().wait_recv()
    for way in range(2):
        field_out[way] = field[...] * other[way] + field_near[...] * wants[way]
        field_copy(way).start()
    send_segment(0)

    for c in load_w[1:]:
        c.wait()
    for c in [load_t] + table_loads:
        c.start()

    def send_many(s, _):
        send_segment(s)
        return 0

    def taken(mine, beside, from_behind, from_ahead):
        return mine * takes_own + beside * takes_near + from_behind * takes_behind + from_ahead * takes_ahead

    def in_copy(d, x):
        return remote(sent.at[d, x], got.at[me, x], in_send.at[d], in_recv.at[me, x], (w, d))

    def self_in(x):
        return pltpu.make_async_copy(sent.at[me, x], got.at[me, x], local_sem.at[x])

    def segment(s):
        group, x = s // SLAB, lax.rem(s, SLAB)
        for j in range(4):
            d = target(group, j)
            for way in range(2):
                pre_copy(way, d, x).wait_recv()
            for yh in range(HIGH):
                sent[d, x, yh] = taken(own[d, x, yh], near[d, x, yh], pre_in[0, d, x, yh], pre_in[1, d, x, yh])

            @pl.when(d != me)
            def _():
                in_copy(d, x).start()

            @pl.when(d == me)
            def _():
                self_in(x).start()

    def ring_field(k, origin=0):
        g = ring(origin)
        n = k + 2 if origin == 0 else k + 6
        return remote(field_all.at[g], field_all.at[g], ring_send.at[n], ring_recv.at[g], (w, ring(k)))

    def field_from(origin):
        g = ring(origin)
        remote(field_all.at[g], field_all.at[g], ring_send.at[0], ring_recv.at[g], (w, ring(1))).wait_recv()

    field_sends = ((1, 0), (-1, 0), (2, 0), (-2, 0), (1, -2), (2, -2), (-1, 2))

    def pick_field():
        for way in range(2):
            field_copy(way).wait_recv()
        field_all[me] = taken(field[...], field_near[...], field_in[0], field_in[1])
        for k, origin in field_sends[:4]:
            ring_field(k, origin).start()

    def pass_field():
        field_from(-2)
        field_from(2)
        for k, origin in field_sends[4:]:
            ring_field(k, origin).start()

    def last_fields():
        for origin in (-1, 1, -3, 3, 4):
            field_from(origin)

    def turn_trial():
        load_t.wait()

        def body(u, _):
            x, yh = u // HIGH, lax.rem(u, HIGH)
            old = trial[x, pl.ds(yh * LOW, LOW)].astype(F32).reshape(LOW * G, LANES)
            turned[u] = old.T.astype(BF)
            return 0

        lax.fori_loop(0, SLAB * HIGH, body, 0)

    def wait_tables():
        for c in table_loads:
            c.wait()

    def field_factors():
        for i in range(RING):
            field_t[:, i * 16:(i + 1) * 16] = field_all[i].astype(F32).T

        def body(i, _):
            for step in range(2):
                rows = field_t[pl.ds(i * 400, 400), :].astype(BF)
                grown = jnp.exp(jnp.dot(rows, spread[step], preferred_element_type=F32))
                for yh in range(HIGH):
                    factor[step, pl.ds(i * 2, 2), :, yh] = cols(grown, yh).reshape(2, SLAB, G, LANES)
            return 0

        lax.fori_loop(0, 4, body, 0)

    def cols(value, yh):
        return value[:, yh * LANES:(yh + 1) * LANES]

    def combined(value, yh, rows):
        c, s = cols(value, yh)[:rows], cols(value, yh)[rows:]
        return c + pltpu.roll(s, HALF, 1) * sign

    def stage_in(x):
        for k in range(1, RING):
            g = ring(k)
            remote(sent.at[g, x], got.at[g, x], in_send.at[g], in_recv.at[g, x], (w, g)).wait_recv()
        self_in(x).wait()
        halves = []
        for h in range(0, RING, 4):
            data = [
                jnp.concatenate([got[g, x, yh].astype(F32) for g in range(h, h + 4)], axis=0).astype(BF)
                for yh in range(HIGH)
            ]
            value = jnp.dot(fz[...], jnp.concatenate(data, axis=1), preferred_element_type=F32)
            halves.append(jnp.concatenate([combined(value, yh, 160).astype(BF) for yh in range(HIGH)], axis=1))
        value = jnp.dot(jnp.concatenate(halves, axis=0), fy[...], preferred_element_type=F32)
        for yh in range(HIGH):
            wb[:, x, yh] = cols(value, yh).reshape(RING, G, LANES)

    def stage_fx():
        def body(i, _):
            at = pl.ds(pl.multiple_of(i * 8, 8), 8)
            data = [wb[:, :, yh, at].reshape(320, LANES).astype(BF) for yh in range(HIGH)]
            value = jnp.dot(fx[...], jnp.concatenate(data, axis=1), preferred_element_type=F32)
            lit = [
                (combined(value, yh, 320) * factor[0, :, :, yh, at].reshape(320, LANES)).astype(BF)
                for yh in range(HIGH)
            ]
            value = jnp.dot(kx[...], jnp.concatenate(lit, axis=1), preferred_element_type=F32)
            for yh in range(HIGH):
                wa[:, :, yh, at] = cols(value, yh).reshape(RING, SLAB, 8, LANES)
            return 0

        lax.fori_loop(0, 5, body, 0)

    def stage_zy():
        def body(i, _):
            halves = []
            for h in range(2):
                data = [wa[2 * i + h, :, yh].reshape(200, LANES).astype(BF) for yh in range(HIGH)]
                halves.append(jnp.dot(kz[...], jnp.concatenate(data, axis=1), preferred_element_type=F32))
            rows = jnp.concatenate(halves, axis=0).astype(BF)
            value = jnp.dot(rows, ky[...], preferred_element_type=F32)
            at = pl.ds(i * 2, 2)
            for yh in range(HIGH):
                lit = cols(value, yh) * factor[1, at, :, yh].reshape(400, LANES)
                wb[at, :, yh] = lit.reshape(2, SLAB, G, LANES)
            return 0

        lax.fori_loop(0, 4, body, 0)

    def stage_bx():
        def body(i, _):
            at = pl.ds(pl.multiple_of(i * 8, 8), 8)
            data = [wb[:, :, yh, at].reshape(320, LANES).astype(BF) for yh in range(HIGH)]
            value = jnp.dot(bx[...], jnp.concatenate(data, axis=1), preferred_element_type=F32)
            for yh in range(HIGH):
                wa[:, :, yh, at] = combined(value, yh, 320).reshape(RING, SLAB, 8, LANES)
            return 0

        lax.fori_loop(0, 5, body, 0)

    def slot(s, _):
        @pl.when(s < SLAB - 1)
        def _():
            shuffle_plane(s + 1)
            send_near(s + 1)
            send_segment(s + 1)

        pl.when(s == 0)(pick_field)

        @pl.when(jnp.logical_or(s == 3, s == 4))
        def _():
            lax.fori_loop(2 * s - 1, 3 * s - 2, send_many, 0)

        @pl.when(s < 2 * SLAB)
        def _():
            segment(s)

        pl.when(s == 1)(wait_tables)
        pl.when(s == 2)(pass_field)

        @pl.when(s == 4)
        def _():
            last_fields()
            field_factors()

        here = s - SLAB * parity

        @pl.when(jnp.logical_and(here >= 2, here <= 6))
        def _():
            stage_in(here - 2)

        pl.when(here == 6)(stage_fx)
        pl.when(here == 7)(stage_zy)
        pl.when(here == 8)(stage_bx)
        return 0

    lax.fori_loop(0, 14, slot, 0)

    def back_copy(g, x):
        return remote(back.at[g, x], late.at[me, x], back_send.at[g], back_recv.at[me, x], (w, g))

    def self_back(x):
        return pltpu.make_async_copy(back.at[me, x], late.at[me, x], local_sem.at[x])

    def stage_bz(x, _):
        data = [wa[:, x, yh].reshape(320, LANES).astype(BF) for yh in range(HIGH)]
        turned_y = jnp.dot(jnp.concatenate(data, axis=1), by[...], preferred_element_type=F32).astype(BF)
        for h in range(2):
            value = jnp.dot(bz[...], turned_y[h * 160:h * 160 + 160], preferred_element_type=F32)
            for yh in range(HIGH):
                back[h * 4:h * 4 + 4, x, yh] = combined(value, yh, 160).reshape(4, G, LANES).astype(BF)
        for k in (4, 3, -3, 2, -2, 1, -1):
            back_copy(ring(k), x).start()
        self_back(x).start()
        return 0

    lax.fori_loop(0, SLAB, stage_bz, 0)

    turn_trial()

    part[...] = jnp.zeros_like(part)

    def store(x):
        return pltpu.make_async_copy(whole.at[x], out_hbm.at[0, x], out_sem.at[x])

    def finish(x, _):
        for k in range(1, RING):
            g = ring(k)
            remote(back.at[g, x], late.at[g, x], back_send.at[g], back_recv.at[g, x], (w, g)).wait_recv()
        self_back(x).wait()

        def body(yh, _):
            moved = swap_blocks([late[d, x, yh] for d in range(RING)], lane)
            for i in range(LOW):
                whole[x, yh * LOW + i] = moved[i]
            new = jnp.concatenate([m.astype(F32) for m in moved], axis=0).astype(BF)
            part[...] += jnp.dot(turned[x * HIGH + yh], new, preferred_element_type=F32)
            return 0

        lax.fori_loop(0, HIGH, body, 0)
        store(x).start()
        return 0

    lax.fori_loop(0, SLAB, finish, 0)

    lower = part[HALF:, :]
    mine = part[:HALF, :] - pltpu.roll(lower, HALF, 1) * sign
    parts[me] = mine.astype(BF)

    def sum_copy(d):
        return remote(parts.at[me], parts.at[me], sum_send.at[d], sum_recv.at[me], (w, d))

    for k in (4, 3, -3, 2, -2, 1, -1):
        sum_copy(ring(k)).start()

    remote(own, near, near_send, near_recv.at[0, 0], sibling).wait_send()
    near_field().wait_send()
    for k, origin in field_sends:
        ring_field(k, origin).wait_send()
    for way in range(2):
        ask(way).wait_send()
        field_copy(way).wait_send()
        remote(pre_out.at[way], pre_in.at[way], pre_send.at[way], pre_recv.at[way, 0, 0], ahead).wait_send()
    for k in range(1, RING):
        d = ring(k)
        remote(sent.at[d], got.at[me], in_send.at[d], in_recv.at[me, 0], (w, d)).wait_send()
        remote(back.at[d], late.at[me], back_send.at[d], back_recv.at[me, 0], (w, d)).wait_send()
    for x in range(SLAB):
        store(x).wait()

    for k in range(1, RING):
        g = ring(k)
        remote(parts.at[g], parts.at[g], sum_send.at[g], sum_recv.at[g], (w, g)).wait_recv()
    total = parts[0].astype(F32)
    for g in range(1, RING):
        total = total + parts[g].astype(F32)
    inter_ref[...] = total * (1.0 / math.sqrt(G**3))
    for k in range(1, RING):
        sum_copy(ring(k)).wait_send()


def hand_over(walkers, inter, walkers_out, inter_out, held, held_inter, in_sem, out_sem):
    steps = [(walkers.at[0, x], held.at[x], walkers_out.at[0, x]) for x in range(SLAB)]
    steps.append((inter, held_inter, inter_out.at[0]))
    inward = [pltpu.make_async_copy(a, b, in_sem.at[i]) for i, (a, b, _) in enumerate(steps)]
    outward = [pltpu.make_async_copy(b, c, out_sem.at[i]) for i, (_, b, c) in enumerate(steps)]
    for c in inward:
        c.start()
    for i, c in enumerate(outward):
        inward[i].wait()
        c.start()
    for c in outward:
        c.wait()


def on_device(walkers_in, trial, fields, sources):
    made = [jnp.asarray(t) for t in tables()]
    anywhere = pl.BlockSpec(memory_space=pl.ANY)
    chunk = (SLAB, HIGH, G, LANES)
    dma = pltpu.SemaphoreType.DMA
    scratch = [
        pltpu.VMEM((SLAB, G, G, LANES), BF),
        pltpu.VMEM((SLAB, G, G, LANES), BF),
        pltpu.VMEM((SLAB * HIGH, LANES, LOW * G), BF),
        pltpu.VMEM((RING,) + chunk, BF),
        pltpu.VMEM((RING,) + chunk, BF),
        pltpu.VMEM((2, RING) + chunk, BF),
        pltpu.VMEM((2, RING) + chunk, BF),
        pltpu.VMEM((RING,) + chunk, BF),
        pltpu.VMEM((RING,) + chunk, BF),
        pltpu.VMEM((RING,) + chunk, F32),
        pltpu.VMEM((RING,) + chunk, F32),
        pltpu.VMEM((2, RING) + chunk, F32),
        pltpu.VMEM((RING,) + chunk, BF),
        pltpu.VMEM((RING,) + chunk, BF),
        pltpu.VMEM((SLAB, 2, G * G), BF),
        pltpu.VMEM((16, G * G), BF),
        pltpu.VMEM((16, G * G), BF),
        pltpu.VMEM((2, 16, G * G), BF),
        pltpu.VMEM((2, 16, G * G), BF),
        pltpu.VMEM((RING, 16, G * G), BF),
        pltpu.VMEM((G * G, RING * 16), F32),
        pltpu.VMEM((8, LANES), F32),
        pltpu.VMEM((2, 8, LANES), F32),
    ]
    scratch += [pltpu.VMEM(t.shape, BF) for t in made]
    scratch += [pltpu.VMEM((LANES, LANES), F32), pltpu.VMEM((RING, HALF, LANES), BF)]
    scratch += [
        dma((3,)), dma((SLAB,)), dma((len(made),)), dma, dma((RING, SLAB)), dma((2,)), dma((2, RING, SLAB)), dma((RING,)), dma((RING, SLAB)),
        dma((RING,)), dma((RING, SLAB)), dma, dma, dma((2,)), dma((2,)), dma((2,)), dma((2,)), dma((9,)),
        dma((RING,)), dma((RING,)), dma((RING,)), dma((SLAB,)), dma((SLAB,)),
    ]
    walkers_out, inter = pl.pallas_call(
        kernel,
        out_shape=(
            jax.ShapeDtypeStruct((1, SLAB, G, G, LANES), BF),
            jax.ShapeDtypeStruct((HALF, LANES), F32),
        ),
        in_specs=[pl.BlockSpec(memory_space=pltpu.SMEM)] + [anywhere] * (3 + len(made)),
        out_specs=(anywhere, pl.BlockSpec(memory_space=pltpu.VMEM)),
        scratch_shapes=scratch,
        compiler_params=pltpu.CompilerParams(
            collective_id=0, has_side_effects=True, vmem_limit_bytes=62 * 2**20
        ),
        name="walkers",
    )(sources, walkers_in, trial, fields.reshape(2, SLAB, G * G).transpose(1, 0, 2), *made)
    return pl.pallas_call(
        hand_over,
        out_shape=(
            jax.ShapeDtypeStruct((1, SLAB, G, G, LANES), BF),
            jax.ShapeDtypeStruct((1, HALF, LANES), F32),
        ),
        in_specs=[anywhere] * 2,
        out_specs=(anywhere,) * 2,
        scratch_shapes=[
            pltpu.VMEM((SLAB, G, G, LANES), BF),
            pltpu.VMEM((HALF, LANES), F32),
            dma((SLAB + 1,)),
            dma((SLAB + 1,)),
        ],
        name="results",
    )(walkers_out, inter)


def solution(mesh):
    placed = (
        P("walk", "grid", None, None, None),
        P("grid", None, None, None),
        P(None, "walk", "grid", None),
        P("walk"),
    )
    return jax.shard_map(
        on_device,
        mesh=mesh,
        in_specs=placed,
        out_specs=(P("walk", "grid", None, None, None), P("walk", None, None)),
        check_vma=False,
    )
```

```python
import functools
import math

import jax
import jax.numpy as jnp
import ml_dtypes
import numpy as np
from jax import lax
from jax.experimental import pallas as pl
from jax.experimental.pallas import tpu as pltpu
from jax.sharding import PartitionSpec as P

MESH = pl.DeviceIdType.MESH
RATE = 0.001
G = 40
SLAB = 5
RING = 8
ORBS = 8
LOW = 8
HIGH = 5
LANES = 128
HALF = 64
BF = jnp.bfloat16
F32 = jnp.float32


def tables():
    n = np.arange(G)
    angle = (n[:, None] * n[None, :] % G) * (2.0 * math.pi / G)
    cos = (np.cos(angle) / math.sqrt(G)).astype(ml_dtypes.bfloat16).astype(np.float64)
    sin = (np.sin(angle) / math.sqrt(G)).astype(ml_dtypes.bfloat16).astype(np.float64)
    signed = np.where(n < G // 2, n, n - G)
    damp = np.exp(-0.5 * RATE * signed**2)
    fc, fs = cos.T * damp[None, :], sin.T * damp[None, :]
    bc, bs = damp[:, None] * cos.T, -damp[:, None] * sin.T
    both = (cos * damp[None, :] ** 2) @ cos.T + (sin * damp[None, :] ** 2) @ sin.T

    def left(parts, before, after):
        grown = [np.kron(np.kron(np.eye(before), p), np.eye(after)) for p in parts]
        return np.concatenate(grown, axis=0)

    def right(c, s):
        c4 = c.T.reshape(HIGH, LOW, HIGH, LOW)
        s4 = s.T.reshape(HIGH, LOW, HIGH, LOW)
        full = np.zeros((HIGH, 2, LOW, ORBS, HIGH, 2, LOW, ORBS))
        for o in range(ORBS):
            full[:, 0, :, o, :, 0, :, o] = c4
            full[:, 1, :, o, :, 1, :, o] = c4
            full[:, 0, :, o, :, 1, :, o] = s4
            full[:, 1, :, o, :, 0, :, o] = -s4
        return full.reshape(HIGH * LANES, HIGH * LANES)

    spread = np.zeros((2, RING, 16, HIGH, 2, LOW, ORBS))
    for step in range(2):
        for y in range(G):
            spread[step, y // SLAB, y % SLAB * 2 + step, y // LOW, :, y % LOW, :] = 1.0
    zero = np.zeros_like(both)
    made = [
        left([fc, fs], 4, 1),
        left([both], SLAB, 1),
        left([bc, bs], 4, 1),
        left([fc, fs], 1, 8),
        left([both], 1, 8),
        left([bc, bs], 1, 8),
        right(fc, fs),
        right(both, zero),
        right(bc, bs),
        spread.reshape(2, RING * 16, HIGH * LANES),
    ]
    return [m.astype(ml_dtypes.bfloat16) for m in made]


def swap_blocks(parts, lane):
    parts = list(parts)
    for bit in range(3):
        shift = 8 << bit
        low = ((lane >> (3 + bit)) & 1) == 0
        for i in range(8):
            if not (i >> bit) & 1:
                j = i | (1 << bit)
                a, b = parts[i], parts[j]
                parts[i] = jnp.where(low, a, pltpu.roll(b, shift, 1))
                parts[j] = jnp.where(low, pltpu.roll(a, LANES - shift, 1), b)
    return parts


def kernel(
    sources, walker_hbm, trial_hbm, field_hbm,
    fz_h, kz_h, bz_h, fx_h, kx_h, bx_h, fy_h, ky_h, by_h, spread_h,
    out_ref, inter_ref,
    whole, trial, turned, own, near, pre_out, pre_in, sent, got, wa, wb, factor, back, late, raw, field, field_near, field_out, field_in, field_all, field_t,
    asked, answer,
    fz, kz, bz, fx, kx, bx, fy, ky, by, spread, part, parts,
    load_sem, plane_sem, table_sem, near_send, near_recv, pre_send, pre_recv, in_send, in_recv, back_send, back_recv,
    fn_send, fn_recv, f_send, f_recv, ask_send, ask_recv, ring_send, ring_recv, sum_send, sum_recv, local_sem,
):
    w = lax.axis_index("walk")
    me = lax.axis_index("grid")
    walks = lax.axis_size("walk")
    core = lax.rem(w, 2)
    parity = lax.rem(me + core, 2)
    distance = jnp.clip(sources[0] - w, -2, 2)
    turn = 1 - 2 * core

    def ring(k):
        return lax.rem(me + k + 2 * RING, RING)

    ahead = (lax.rem(w + 2, walks), me)
    behind = (lax.rem(w - 2 + walks, walks), me)
    sibling = (w + 1 - 2 * core, me)
    def remote(src, dst, ssem, rsem, device):
        return pltpu.make_async_remote_copy(
            src_ref=src, dst_ref=dst, send_sem=ssem, recv_sem=rsem, device_id=device, device_id_type=MESH
        )

    barrier = pltpu.get_barrier_semaphore()
    for k in range(1, RING):
        pl.semaphore_signal(barrier, inc=1, device_id=(w, ring(k)), device_id_type=MESH)
    for device in (ahead, behind, sibling):
        pl.semaphore_signal(barrier, inc=1, device_id=device, device_id_type=MESH)

    load_f = pltpu.make_async_copy(field_hbm, raw, load_sem.at[1])
    load_f.start()
    load_w = [pltpu.make_async_copy(walker_hbm.at[0, x], whole.at[x], plane_sem.at[x]) for x in range(SLAB)]
    for c in load_w:
        c.start()

    lane = lax.broadcasted_iota(jnp.int32, (G, LANES), 1)
    sign = jnp.where(lax.broadcasted_iota(jnp.int32, (1, LANES), 1) < HALF, -1.0, 1.0).astype(F32)

    def flag(condition):
        return condition.astype(F32).astype(BF)

    to_sibling = 1 - 2 * core
    takes_own = flag(distance == 0)
    takes_near = flag(distance == to_sibling)
    takes_behind = flag(jnp.logical_or(distance == -2, distance == -to_sibling) & (distance < 0))
    takes_ahead = flag(jnp.logical_or(distance == 2, distance == -to_sibling) & (distance > 0))

    def target(group, j):
        step = jnp.where(parity == group, 2 * j + 2, 2 * j + 1)
        return lax.rem(me + turn * step + 2 * RING, RING)

    def near_copy(d, x):
        return remote(own.at[d, x], near.at[d, x], near_send, near_recv.at[d, x], sibling)

    def pre_copy(way, d, x):
        device = ahead if way == 0 else behind
        return remote(pre_out.at[way, d, x], pre_in.at[way, d, x], pre_send.at[way], pre_recv.at[way, d, x], device)

    def shuffle(x, yh):
        rows = [whole[x, yh * LOW + i] for i in range(LOW)]
        moved = swap_blocks(rows, lane)
        for d in range(RING):
            own[d, x, yh] = moved[d]

    def shuffle_plane(x):
        for yh in range(HIGH):
            shuffle(x, yh)

    def ask(way):
        device = behind if way == 0 else ahead
        return remote(asked, answer.at[way], ask_send.at[way], ask_recv.at[way], device)

    def near_field():
        return remote(field, field_near, fn_send, fn_recv, sibling)

    def field_copy(way):
        device = ahead if way == 0 else behind
        return remote(field_out.at[way], field_in.at[way], f_send.at[way], f_recv.at[way], device)

    asked[...] = jnp.full(asked.shape, distance.astype(F32), F32)
    load_f.wait()
    rows = [raw[y].astype(F32) for y in range(SLAB)] + [jnp.zeros((6, G * G), F32)]
    field[...] = jnp.concatenate(rows, axis=0).astype(BF)
    load_w[0].wait()
    shuffle_plane(0)
    pl.semaphore_wait(barrier, RING - 1 + 3)
    near_field().start()
    for way in range(2):
        ask(way).start()

    def send_near(x):
        for j in range(4):
            for group in (1, 0):
                near_copy(target(group, j), x).start()

    def send_segment(s):
        group, x = s // SLAB, lax.rem(s, SLAB)
        for j in range(4):
            d = target(group, j)
            near_copy(d, x).wait_recv()
            for way in range(2):
                for yh in range(HIGH):
                    pre_out[way, d, x, yh] = own[d, x, yh] * other[way] + near[d, x, yh] * wants[way]
                pre_copy(way, d, x).start()

    send_near(0)
    load_t = pltpu.make_async_copy(trial_hbm, trial, load_sem.at[2])
    table_loads = []
    pairs = ((fz_h, fz), (kz_h, kz), (bz_h, bz), (fx_h, fx), (kx_h, kx), (bx_h, bx), (fy_h, fy), (ky_h, ky), (by_h, by),
             (spread_h, spread))
    for i, (src, dst) in enumerate(pairs):
        c = pltpu.make_async_copy(src, dst, table_sem.at[i])
        table_loads.append(c)
    for way in range(2):
        ask(way).wait_recv()
    wants = [flag(answer[0, 0, 0] == -1.0), flag(answer[1, 0, 0] == 1.0)]
    other = [flag(answer[0, 0, 0] != -1.0), flag(answer[1, 0, 0] != 1.0)]

    near_field().wait_recv()
    for way in range(2):
        field_out[way] = field[...] * other[way] + field_near[...] * wants[way]
        field_copy(way).start()
    send_segment(0)

    for c in load_w[1:]:
        c.wait()
    for c in [load_t] + table_loads:
        c.start()

    def send_many(s, _):
        send_segment(s)
        return 0

    def taken(mine, beside, from_behind, from_ahead):
        return mine * takes_own + beside * takes_near + from_behind * takes_behind + from_ahead * takes_ahead

    def in_copy(d, x):
        return remote(sent.at[d, x], got.at[me, x], in_send.at[d], in_recv.at[me, x], (w, d))

    def self_in(x):
        return pltpu.make_async_copy(sent.at[me, x], got.at[me, x], local_sem.at[x])

    def segment(s):
        group, x = s // SLAB, lax.rem(s, SLAB)
        for j in range(4):
            d = target(group, j)
            for way in range(2):
                pre_copy(way, d, x).wait_recv()
            for yh in range(HIGH):
                sent[d, x, yh] = taken(own[d, x, yh], near[d, x, yh], pre_in[0, d, x, yh], pre_in[1, d, x, yh])

            @pl.when(d != me)
            def _():
                in_copy(d, x).start()

            @pl.when(d == me)
            def _():
                self_in(x).start()

    def ring_field(k, origin=0):
        g = ring(origin)
        n = k + 2 if origin == 0 else k + 6
        return remote(field_all.at[g], field_all.at[g], ring_send.at[n], ring_recv.at[g], (w, ring(k)))

    def field_from(origin):
        g = ring(origin)
        remote(field_all.at[g], field_all.at[g], ring_send.at[0], ring_recv.at[g], (w, ring(1))).wait_recv()

    field_sends = ((1, 0), (-1, 0), (2, 0), (-2, 0), (1, -2), (2, -2), (-1, 2))

    def pick_field():
        for way in range(2):
            field_copy(way).wait_recv()
        field_all[me] = taken(field[...], field_near[...], field_in[0], field_in[1])
        for k, origin in field_sends[:4]:
            ring_field(k, origin).start()

    def pass_field():
        field_from(-2)
        field_from(2)
        for k, origin in field_sends[4:]:
            ring_field(k, origin).start()

    def last_fields():
        for origin in (-1, 1, -3, 3, 4):
            field_from(origin)

    def turn_trial():
        load_t.wait()

        def body(u, _):
            x, yh = u // HIGH, lax.rem(u, HIGH)
            old = trial[x, pl.ds(yh * LOW, LOW)].astype(F32).reshape(LOW * G, LANES)
            turned[u] = old.T.astype(BF)
            return 0

        lax.fori_loop(0, SLAB * HIGH, body, 0)

    def wait_tables():
        for c in table_loads:
            c.wait()

    def field_factors():
        for i in range(RING):
            field_t[:, i * 16:(i + 1) * 16] = field_all[i].astype(F32).T

        def body(i, _):
            for step in range(2):
                rows = field_t[pl.ds(i * 400, 400), :].astype(BF)
                grown = jnp.exp(jnp.dot(rows, spread[step], preferred_element_type=F32))
                for yh in range(HIGH):
                    factor[step, pl.ds(i * 2, 2), :, yh] = cols(grown, yh).reshape(2, SLAB, G, LANES)
            return 0

        lax.fori_loop(0, 4, body, 0)

    def cols(value, yh):
        return value[:, yh * LANES:(yh + 1) * LANES]

    def combined(value, yh, rows):
        c, s = cols(value, yh)[:rows], cols(value, yh)[rows:]
        return c + pltpu.roll(s, HALF, 1) * sign

    def stage_in(x):
        for k in range(1, RING):
            g = ring(k)
            remote(sent.at[g, x], got.at[g, x], in_send.at[g], in_recv.at[g, x], (w, g)).wait_recv()
        self_in(x).wait()
        halves = []
        for h in range(0, RING, 4):
            data = [
                jnp.concatenate([got[g, x, yh].astype(F32) for g in range(h, h + 4)], axis=0).astype(BF)
                for yh in range(HIGH)
            ]
            value = jnp.dot(fz[...], jnp.concatenate(data, axis=1), preferred_element_type=F32)
            halves.append(jnp.concatenate([combined(value, yh, 160).astype(BF) for yh in range(HIGH)], axis=1))
        value = jnp.dot(jnp.concatenate(halves, axis=0), fy[...], preferred_element_type=F32)
        for yh in range(HIGH):
            wb[:, x, yh] = cols(value, yh).reshape(RING, G, LANES)

    def stage_fx():
        def body(i, _):
            at = pl.ds(pl.multiple_of(i * 8, 8), 8)
            data = [wb[:, :, yh, at].reshape(320, LANES).astype(BF) for yh in range(HIGH)]
            value = jnp.dot(fx[...], jnp.concatenate(data, axis=1), preferred_element_type=F32)
            lit = [
                (combined(value, yh, 320) * factor[0, :, :, yh, at].reshape(320, LANES)).astype(BF)
                for yh in range(HIGH)
            ]
            value = jnp.dot(kx[...], jnp.concatenate(lit, axis=1), preferred_element_type=F32)
            for yh in range(HIGH):
                wa[:, :, yh, at] = cols(value, yh).reshape(RING, SLAB, 8, LANES)
            return 0

        lax.fori_loop(0, 5, body, 0)

    def stage_zy():
        def body(i, _):
            halves = []
            for h in range(2):
                data = [wa[2 * i + h, :, yh].reshape(200, LANES).astype(BF) for yh in range(HIGH)]
                halves.append(jnp.dot(kz[...], jnp.concatenate(data, axis=1), preferred_element_type=F32))
            rows = jnp.concatenate(halves, axis=0).astype(BF)
            value = jnp.dot(rows, ky[...], preferred_element_type=F32)
            at = pl.ds(i * 2, 2)
            for yh in range(HIGH):
                lit = cols(value, yh) * factor[1, at, :, yh].reshape(400, LANES)
                wb[at, :, yh] = lit.reshape(2, SLAB, G, LANES)
            return 0

        lax.fori_loop(0, 4, body, 0)

    def stage_bx():
        def body(i, _):
            at = pl.ds(pl.multiple_of(i * 8, 8), 8)
            data = [wb[:, :, yh, at].reshape(320, LANES).astype(BF) for yh in range(HIGH)]
            value = jnp.dot(bx[...], jnp.concatenate(data, axis=1), preferred_element_type=F32)
            for yh in range(HIGH):
                wa[:, :, yh, at] = combined(value, yh, 320).reshape(RING, SLAB, 8, LANES)
            return 0

        lax.fori_loop(0, 5, body, 0)

    def slot(s, _):
        @pl.when(s < SLAB - 1)
        def _():
            shuffle_plane(s + 1)
            send_near(s + 1)
            send_segment(s + 1)

        pl.when(s == 0)(pick_field)

        @pl.when(jnp.logical_or(s == 3, s == 4))
        def _():
            lax.fori_loop(2 * s - 1, 3 * s - 2, send_many, 0)

        @pl.when(s < 2 * SLAB)
        def _():
            segment(s)

        pl.when(s == 1)(wait_tables)
        pl.when(s == 2)(pass_field)

        @pl.when(s == 4)
        def _():
            last_fields()
            field_factors()

        here = s - SLAB * parity

        @pl.when(jnp.logical_and(here >= 2, here <= 6))
        def _():
            stage_in(here - 2)

        pl.when(here == 6)(stage_fx)
        pl.when(here == 7)(stage_zy)
        pl.when(here == 8)(stage_bx)
        return 0

    lax.fori_loop(0, 14, slot, 0)

    def back_copy(g, x):
        return remote(back.at[g, x], late.at[me, x], back_send.at[g], back_recv.at[me, x], (w, g))

    def self_back(x):
        return pltpu.make_async_copy(back.at[me, x], late.at[me, x], local_sem.at[x])

    def stage_bz(x, _):
        data = [wa[:, x, yh].reshape(320, LANES).astype(BF) for yh in range(HIGH)]
        turned_y = jnp.dot(jnp.concatenate(data, axis=1), by[...], preferred_element_type=F32).astype(BF)
        for h in range(2):
            value = jnp.dot(bz[...], turned_y[h * 160:h * 160 + 160], preferred_element_type=F32)
            for yh in range(HIGH):
                back[h * 4:h * 4 + 4, x, yh] = combined(value, yh, 160).reshape(4, G, LANES).astype(BF)
        for k in (4, 3, -3, 2, -2, 1, -1):
            back_copy(ring(k), x).start()
        self_back(x).start()
        return 0

    lax.fori_loop(0, SLAB, stage_bz, 0)

    turn_trial()

    part[...] = jnp.zeros_like(part)

    def finish(x, _):
        for k in range(1, RING):
            g = ring(k)
            remote(back.at[g, x], late.at[g, x], back_send.at[g], back_recv.at[g, x], (w, g)).wait_recv()
        self_back(x).wait()

        total = part[...]
        for yh in range(HIGH):
            moved = swap_blocks([late[d, x, yh] for d in range(RING)], lane)
            for i in range(LOW):
                out_ref[x, yh * LOW + i] = moved[i]
            new = jnp.concatenate([m.astype(F32) for m in moved], axis=0).astype(BF)
            total = total + jnp.dot(turned[x * HIGH + yh], new, preferred_element_type=F32)
        part[...] = total
        return 0

    lax.fori_loop(0, SLAB, finish, 0)

    lower = part[HALF:, :]
    mine = part[:HALF, :] - pltpu.roll(lower, HALF, 1) * sign
    parts[me] = mine.astype(BF)

    def sum_copy(d):
        return remote(parts.at[me], parts.at[me], sum_send.at[d], sum_recv.at[me], (w, d))

    for k in (4, 3, -3, 2, -2, 1, -1):
        sum_copy(ring(k)).start()

    remote(own, near, near_send, near_recv.at[0, 0], sibling).wait_send()
    near_field().wait_send()
    for k, origin in field_sends:
        ring_field(k, origin).wait_send()
    for way in range(2):
        ask(way).wait_send()
        field_copy(way).wait_send()
        remote(pre_out.at[way], pre_in.at[way], pre_send.at[way], pre_recv.at[way, 0, 0], ahead).wait_send()
    for k in range(1, RING):
        d = ring(k)
        remote(sent.at[d], got.at[me], in_send.at[d], in_recv.at[me, 0], (w, d)).wait_send()
        remote(back.at[d], late.at[me], back_send.at[d], back_recv.at[me, 0], (w, d)).wait_send()

    for k in range(1, RING):
        g = ring(k)
        remote(parts.at[g], parts.at[g], sum_send.at[g], sum_recv.at[g], (w, g)).wait_recv()
    total = parts[0].astype(F32)
    for g in range(1, RING):
        total = total + parts[g].astype(F32)
    inter_ref[...] = total * (1.0 / math.sqrt(G**3))
    for k in range(1, RING):
        sum_copy(ring(k)).wait_send()


def hand_over(walkers, inter, walkers_out, inter_out, sem):
    copies = [pltpu.make_async_copy(walkers.at[x], walkers_out.at[0, x], sem.at[x]) for x in range(SLAB)]
    copies.append(pltpu.make_async_copy(inter, inter_out.at[0], sem.at[SLAB]))
    for c in copies:
        c.start()
    for c in copies:
        c.wait()


def on_device(walkers_in, trial, fields, sources):
    made = [jnp.asarray(t) for t in tables()]
    anywhere = pl.BlockSpec(memory_space=pl.ANY)
    chunk = (SLAB, HIGH, G, LANES)
    dma = pltpu.SemaphoreType.DMA
    scratch = [
        pltpu.VMEM((SLAB, G, G, LANES), BF),
        pltpu.VMEM((SLAB, G, G, LANES), BF),
        pltpu.VMEM((SLAB * HIGH, LANES, LOW * G), BF),
        pltpu.VMEM((RING,) + chunk, BF),
        pltpu.VMEM((RING,) + chunk, BF),
        pltpu.VMEM((2, RING) + chunk, BF),
        pltpu.VMEM((2, RING) + chunk, BF),
        pltpu.VMEM((RING,) + chunk, BF),
        pltpu.VMEM((RING,) + chunk, BF),
        pltpu.VMEM((RING,) + chunk, F32),
        pltpu.VMEM((RING,) + chunk, F32),
        pltpu.VMEM((2, RING) + chunk, F32),
        pltpu.VMEM((RING,) + chunk, BF),
        pltpu.VMEM((RING,) + chunk, BF),
        pltpu.VMEM((SLAB, 2, G * G), BF),
        pltpu.VMEM((16, G * G), BF),
        pltpu.VMEM((16, G * G), BF),
        pltpu.VMEM((2, 16, G * G), BF),
        pltpu.VMEM((2, 16, G * G), BF),
        pltpu.VMEM((RING, 16, G * G), BF),
        pltpu.VMEM((G * G, RING * 16), F32),
        pltpu.VMEM((8, LANES), F32),
        pltpu.VMEM((2, 8, LANES), F32),
    ]
    scratch += [pltpu.VMEM(t.shape, BF) for t in made]
    scratch += [pltpu.VMEM((LANES, LANES), F32), pltpu.VMEM((RING, HALF, LANES), BF)]
    scratch += [
        dma((3,)), dma((SLAB,)), dma((len(made),)), dma, dma((RING, SLAB)), dma((2,)), dma((2, RING, SLAB)), dma((RING,)), dma((RING, SLAB)),
        dma((RING,)), dma((RING, SLAB)), dma, dma, dma((2,)), dma((2,)), dma((2,)), dma((2,)), dma((9,)),
        dma((RING,)), dma((RING,)), dma((RING,)), dma((SLAB,)),
    ]
    walkers_out, inter = pl.pallas_call(
        kernel,
        out_shape=(pltpu.VMEM((SLAB, G, G, LANES), BF), pltpu.VMEM((HALF, LANES), F32)),
        in_specs=[pl.BlockSpec(memory_space=pltpu.SMEM)] + [anywhere] * (3 + len(made)),
        out_specs=(pl.BlockSpec(memory_space=pltpu.VMEM),) * 2,
        scratch_shapes=scratch,
        compiler_params=pltpu.CompilerParams(
            collective_id=0, has_side_effects=True, vmem_limit_bytes=58 * 2**20
        ),
        name="walkers",
    )(sources, walkers_in, trial, fields.reshape(2, SLAB, G * G).transpose(1, 0, 2), *made)
    return pl.pallas_call(
        hand_over,
        out_shape=(
            jax.ShapeDtypeStruct((1, SLAB, G, G, LANES), BF),
            jax.ShapeDtypeStruct((1, HALF, LANES), F32),
        ),
        in_specs=[pl.BlockSpec(memory_space=pltpu.VMEM)] * 2,
        out_specs=(anywhere,) * 2,
        scratch_shapes=[dma((SLAB + 1,))],
        name="results",
    )(*(pltpu.with_memory_space_constraint(a, pltpu.VMEM) for a in (walkers_out, inter)))


def solution(mesh):
    placed = (
        P("walk", "grid", None, None, None),
        P("grid", None, None, None),
        P(None, "walk", "grid", None),
        P("walk"),
    )
    return jax.shard_map(
        on_device,
        mesh=mesh,
        in_specs=placed,
        out_specs=(P("walk", "grid", None, None, None), P("walk", None, None)),
        check_vma=False,
    )
```

```python
import functools
import math

import jax
import jax.numpy as jnp
import ml_dtypes
import numpy as np
from jax import lax
from jax.experimental import pallas as pl
from jax.experimental.pallas import tpu as pltpu
from jax.sharding import PartitionSpec as P

MESH = pl.DeviceIdType.MESH
RATE = 0.001
G = 40
SLAB = 5
RING = 8
ORBS = 8
LOW = 8
HIGH = 5
LANES = 128
QUARTER = 400
EXTRA = 1664
WIDE = EXTRA + 512
HALF = 64
BF = jnp.bfloat16
F32 = jnp.float32


def tables():
    n = np.arange(G)
    angle = (n[:, None] * n[None, :] % G) * (2.0 * math.pi / G)
    cos = (np.cos(angle) / math.sqrt(G)).astype(ml_dtypes.bfloat16).astype(np.float64)
    sin = (np.sin(angle) / math.sqrt(G)).astype(ml_dtypes.bfloat16).astype(np.float64)
    signed = np.where(n < G // 2, n, n - G)
    damp = np.exp(-0.5 * RATE * signed**2)
    fc, fs = cos.T * damp[None, :], sin.T * damp[None, :]
    bc, bs = damp[:, None] * cos.T, -damp[:, None] * sin.T
    both = (cos * damp[None, :] ** 2) @ cos.T + (sin * damp[None, :] ** 2) @ sin.T

    def left(parts, before, after):
        grown = [np.kron(np.kron(np.eye(before), p), np.eye(after)) for p in parts]
        return np.concatenate(grown, axis=0)

    def right(c, s):
        c4 = c.T.reshape(HIGH, LOW, HIGH, LOW)
        s4 = s.T.reshape(HIGH, LOW, HIGH, LOW)
        full = np.zeros((HIGH, 2, LOW, ORBS, HIGH, 2, LOW, ORBS))
        for o in range(ORBS):
            full[:, 0, :, o, :, 0, :, o] = c4
            full[:, 1, :, o, :, 1, :, o] = c4
            full[:, 0, :, o, :, 1, :, o] = s4
            full[:, 1, :, o, :, 0, :, o] = -s4
        return full.reshape(HIGH * LANES, HIGH * LANES)

    spread = np.zeros((4, 2, 2, RING, 8, HIGH, 2, LOW, ORBS))
    for quarter in range(4):
        for step in range(2):
            for y in range(G):
                row = y % SLAB * 2 + step
                extra = row // 8
                spread[quarter, step, extra, y // SLAB, 4 * step + quarter if extra else row, y // LOW, :, y % LOW, :] = 1.0
    zero = np.zeros_like(both)
    made = [
        left([fc, fs], 4, 1),
        left([both], SLAB, 1),
        left([bc, bs], 4, 1),
        left([fc, fs], 1, 8),
        left([both], 1, 8),
        left([bc, bs], 1, 8),
        right(fc, fs),
        right(both, zero),
        right(bc, bs),
        spread.reshape(4, 2, LANES, HIGH * LANES),
    ]
    return [m.astype(ml_dtypes.bfloat16) for m in made]


def swap_blocks(parts, lane):
    parts = list(parts)
    for bit in range(3):
        shift = 8 << bit
        low = ((lane >> (3 + bit)) & 1) == 0
        for i in range(8):
            if not (i >> bit) & 1:
                j = i | (1 << bit)
                a, b = parts[i], parts[j]
                parts[i] = jnp.where(low, a, pltpu.roll(b, shift, 1))
                parts[j] = jnp.where(low, pltpu.roll(a, LANES - shift, 1), b)
    return parts


def kernel(
    sources, walker_hbm, trial_hbm, field_hbm,
    fz_h, kz_h, bz_h, fx_h, kx_h, bx_h, fy_h, ky_h, by_h, spread_h,
    out_ref, inter_ref,
    whole, trial, turned, own, near, pre_out, pre_in, sent, got, wa, wb, factor, back, late, raw, field, field_near, field_out, field_in, field_all, field_t,
    asked, answer,
    fz, kz, bz, fx, kx, bx, fy, ky, by, spread, part, parts,
    load_sem, plane_sem, table_sem, near_send, near_recv, pre_send, pre_recv, in_send, in_recv, back_send, back_recv,
    fn_send, fn_recv, f_send, f_recv, ask_send, ask_recv, ring_send, ring_recv, sum_send, sum_recv, local_sem,
):
    w = lax.axis_index("walk")
    me = lax.axis_index("grid")
    walks = lax.axis_size("walk")
    core = lax.rem(w, 2)
    parity = lax.rem(me + core, 2)
    distance = jnp.clip(sources[0] - w, -2, 2)
    turn = 1 - 2 * core

    def ring(k):
        return lax.rem(me + k + 2 * RING, RING)

    ahead = (lax.rem(w + 2, walks), me)
    behind = (lax.rem(w - 2 + walks, walks), me)
    sibling = (w + 1 - 2 * core, me)
    def remote(src, dst, ssem, rsem, device):
        return pltpu.make_async_remote_copy(
            src_ref=src, dst_ref=dst, send_sem=ssem, recv_sem=rsem, device_id=device, device_id_type=MESH
        )

    barrier = pltpu.get_barrier_semaphore()
    for k in range(1, RING):
        pl.semaphore_signal(barrier, inc=1, device_id=(w, ring(k)), device_id_type=MESH)
    for device in (ahead, behind, sibling):
        pl.semaphore_signal(barrier, inc=1, device_id=device, device_id_type=MESH)

    load_f = pltpu.make_async_copy(field_hbm, raw, load_sem.at[1])
    load_f.start()
    load_w = [pltpu.make_async_copy(walker_hbm.at[0, x], whole.at[x], plane_sem.at[x]) for x in range(SLAB)]
    for c in load_w:
        c.start()

    lane = lax.broadcasted_iota(jnp.int32, (G, LANES), 1)
    sign = jnp.where(lax.broadcasted_iota(jnp.int32, (1, LANES), 1) < HALF, -1.0, 1.0).astype(F32)

    def flag(condition):
        return condition.astype(F32).astype(BF)

    to_sibling = 1 - 2 * core
    takes_own = flag(distance == 0)
    takes_near = flag(distance == to_sibling)
    takes_behind = flag(jnp.logical_or(distance == -2, distance == -to_sibling) & (distance < 0))
    takes_ahead = flag(jnp.logical_or(distance == 2, distance == -to_sibling) & (distance > 0))

    def target(group, j):
        step = jnp.where(parity == group, 2 * j + 2, 2 * j + 1)
        return lax.rem(me + turn * step + 2 * RING, RING)

    def near_copy(d, x):
        return remote(own.at[d, x], near.at[d, x], near_send, near_recv.at[d, x], sibling)

    def pre_copy(way, d, x):
        device = ahead if way == 0 else behind
        return remote(pre_out.at[way, d, x], pre_in.at[way, d, x], pre_send.at[way], pre_recv.at[way, d, x], device)

    def shuffle(x, yh):
        rows = [whole[x, yh * LOW + i] for i in range(LOW)]
        moved = swap_blocks(rows, lane)
        for d in range(RING):
            own[d, x, yh] = moved[d]

    def shuffle_plane(x):
        for yh in range(HIGH):
            shuffle(x, yh)

    def ask(way):
        device = behind if way == 0 else ahead
        return remote(asked, answer.at[way], ask_send.at[way], ask_recv.at[way], device)

    def near_field():
        return remote(field, field_near, fn_send, fn_recv, sibling)

    def field_copy(way):
        device = ahead if way == 0 else behind
        return remote(field_out.at[way], field_in.at[way], f_send.at[way], f_recv.at[way], device)

    asked[...] = jnp.full(asked.shape, distance.astype(F32), F32)
    load_w[0].wait()
    shuffle_plane(0)
    pl.semaphore_wait(barrier, RING - 1 + 3)

    def send_near(x):
        for group in (1, 0):
            for j in range(4):
                near_copy(target(group, j), x).start()

    def send_segment(s):
        group, x = s // SLAB, lax.rem(s, SLAB)
        for j in range(4):
            d = target(group, j)
            near_copy(d, x).wait_recv()
            for way in range(2):
                for yh in range(HIGH):
                    pre_out[way, d, x, yh] = own[d, x, yh] * other[way] + near[d, x, yh] * wants[way]
                pre_copy(way, d, x).start()

    for way in range(2):
        ask(way).start()
    send_near(0)
    load_f.wait()
    first = jnp.concatenate([raw[y].astype(F32) for y in range(4)], axis=0)
    field[:, :EXTRA] = jnp.concatenate([first, jnp.zeros((8, EXTRA - G * G), F32)], axis=1).astype(BF)
    last = raw[4].astype(F32)
    quarters = [last[r:r + 1, q * QUARTER:(q + 1) * QUARTER] for r in range(2) for q in range(4)]
    extra = jnp.concatenate([jnp.concatenate(quarters, axis=0), jnp.zeros((8, 512 - QUARTER), F32)], axis=1)
    field[:, EXTRA:] = extra.astype(BF)
    near_field().start()
    load_t = pltpu.make_async_copy(trial_hbm, trial, load_sem.at[2])
    table_loads = []
    pairs = ((fz_h, fz), (kz_h, kz), (bz_h, bz), (fx_h, fx), (kx_h, kx), (bx_h, bx), (fy_h, fy), (ky_h, ky), (by_h, by),
             (spread_h, spread))
    for i, (src, dst) in enumerate(pairs):
        c = pltpu.make_async_copy(src, dst, table_sem.at[i])
        table_loads.append(c)
    for way in range(2):
        ask(way).wait_recv()
    wants = [flag(answer[0, 0, 0] == -1.0), flag(answer[1, 0, 0] == 1.0)]
    other = [flag(answer[0, 0, 0] != -1.0), flag(answer[1, 0, 0] != 1.0)]

    send_segment(0)
    near_field().wait_recv()
    for way in range(2):
        field_out[way] = field[...] * other[way] + field_near[...] * wants[way]
        field_copy(way).start()

    for c in load_w[1:]:
        c.wait()
    for c in [load_t] + table_loads:
        c.start()

    def send_many(s, _):
        send_segment(s)
        return 0

    def taken(mine, beside, from_behind, from_ahead):
        return mine * takes_own + beside * takes_near + from_behind * takes_behind + from_ahead * takes_ahead

    def in_copy(d, x):
        return remote(sent.at[d, x], got.at[me, x], in_send.at[d], in_recv.at[me, x], (w, d))

    def self_in(x):
        return pltpu.make_async_copy(sent.at[me, x], got.at[me, x], local_sem.at[x])

    def segment(s):
        group, x = s // SLAB, lax.rem(s, SLAB)
        for j in range(4):
            d = target(group, j)
            for way in range(2):
                pre_copy(way, d, x).wait_recv()
            for yh in range(HIGH):
                sent[d, x, yh] = taken(own[d, x, yh], near[d, x, yh], pre_in[0, d, x, yh], pre_in[1, d, x, yh])

            @pl.when(d != me)
            def _():
                in_copy(d, x).start()

            @pl.when(d == me)
            def _():
                self_in(x).start()

    def ring_field(k, origin=0):
        g = ring(origin)
        n = k + 2 if origin == 0 else k + 6
        return remote(field_all.at[g], field_all.at[g], ring_send.at[n], ring_recv.at[g], (w, ring(k)))

    def field_from(origin):
        g = ring(origin)
        remote(field_all.at[g], field_all.at[g], ring_send.at[0], ring_recv.at[g], (w, ring(1))).wait_recv()

    field_sends = ((1, 0), (-1, 0), (2, 0), (-2, 0), (1, -2), (2, -2), (-1, 2))

    def pick_field():
        for way in range(2):
            field_copy(way).wait_recv()
        field_all[me] = taken(field[...], field_near[...], field_in[0], field_in[1])
        for k, origin in field_sends[:4]:
            ring_field(k, origin).start()

    def pass_field():
        field_from(-2)
        field_from(2)
        for k, origin in field_sends[4:]:
            ring_field(k, origin).start()

    def last_fields():
        for origin in (-1, 1, -3, 3, 4):
            field_from(origin)

    def turn_trial():
        load_t.wait()

        def body(u, _):
            x, yh = u // HIGH, lax.rem(u, HIGH)
            old = trial[x, pl.ds(yh * LOW, LOW)].astype(F32).reshape(LOW * G, LANES)
            turned[u] = old.T.astype(BF)
            return 0

        lax.fori_loop(0, SLAB * HIGH, body, 0)

    def wait_tables():
        for c in table_loads:
            c.wait()

    def field_factors():
        for i in range(RING):
            field_t[:, i * 8:(i + 1) * 8] = field_all[i].astype(F32).T

        def body(i, _):
            for step in range(2):
                rows = [field_t[pl.ds(i * QUARTER, QUARTER), :HALF], field_t[EXTRA:EXTRA + QUARTER, :HALF]]
                rows = jnp.concatenate(rows, axis=1).astype(BF)
                grown = jnp.exp(jnp.dot(rows, spread[i, step], preferred_element_type=F32))
                for yh in range(HIGH):
                    factor[step, pl.ds(i * 2, 2), :, yh] = cols(grown, yh).reshape(2, SLAB, G, LANES)
            return 0

        lax.fori_loop(0, 4, body, 0)

    def cols(value, yh):
        return value[:, yh * LANES:(yh + 1) * LANES]

    def combined(value, yh, rows):
        c, s = cols(value, yh)[:rows], cols(value, yh)[rows:]
        return c + pltpu.roll(s, HALF, 1) * sign

    def stage_in(x):
        for k in range(1, RING):
            g = ring(k)
            remote(sent.at[g, x], got.at[g, x], in_send.at[g], in_recv.at[g, x], (w, g)).wait_recv()
        self_in(x).wait()
        halves = []
        for h in range(0, RING, 4):
            data = [
                jnp.concatenate([got[g, x, yh].astype(F32) for g in range(h, h + 4)], axis=0).astype(BF)
                for yh in range(HIGH)
            ]
            value = jnp.dot(fz[...], jnp.concatenate(data, axis=1), preferred_element_type=F32)
            halves.append(jnp.concatenate([combined(value, yh, 160).astype(BF) for yh in range(HIGH)], axis=1))
        value = jnp.dot(jnp.concatenate(halves, axis=0), fy[...], preferred_element_type=F32)
        for yh in range(HIGH):
            wb[:, x, yh] = cols(value, yh).reshape(RING, G, LANES)

    def stage_fx():
        def body(i, _):
            at = pl.ds(pl.multiple_of(i * 8, 8), 8)
            data = [wb[:, :, yh, at].reshape(320, LANES).astype(BF) for yh in range(HIGH)]
            value = jnp.dot(fx[...], jnp.concatenate(data, axis=1), preferred_element_type=F32)
            lit = [
                (combined(value, yh, 320) * factor[0, :, :, yh, at].reshape(320, LANES)).astype(BF)
                for yh in range(HIGH)
            ]
            value = jnp.dot(kx[...], jnp.concatenate(lit, axis=1), preferred_element_type=F32)
            for yh in range(HIGH):
                wa[:, :, yh, at] = cols(value, yh).reshape(RING, SLAB, 8, LANES)
            return 0

        lax.fori_loop(0, 5, body, 0)

    def stage_zy():
        def body(i, _):
            halves = []
            for h in range(2):
                data = [wa[2 * i + h, :, yh].reshape(200, LANES).astype(BF) for yh in range(HIGH)]
                halves.append(jnp.dot(kz[...], jnp.concatenate(data, axis=1), preferred_element_type=F32))
            rows = jnp.concatenate(halves, axis=0).astype(BF)
            value = jnp.dot(rows, ky[...], preferred_element_type=F32)
            at = pl.ds(i * 2, 2)
            for yh in range(HIGH):
                lit = cols(value, yh) * factor[1, at, :, yh].reshape(400, LANES)
                wb[at, :, yh] = lit.reshape(2, SLAB, G, LANES)
            return 0

        lax.fori_loop(0, 4, body, 0)

    def stage_bx():
        def body(i, _):
            at = pl.ds(pl.multiple_of(i * 8, 8), 8)
            data = [wb[:, :, yh, at].reshape(320, LANES).astype(BF) for yh in range(HIGH)]
            value = jnp.dot(bx[...], jnp.concatenate(data, axis=1), preferred_element_type=F32)
            for yh in range(HIGH):
                wa[:, :, yh, at] = combined(value, yh, 320).reshape(RING, SLAB, 8, LANES)
            return 0

        lax.fori_loop(0, 5, body, 0)

    def slot(s, _):
        @pl.when(s < SLAB - 1)
        def _():
            shuffle_plane(s + 1)
            send_near(s + 1)
            send_segment(s + 1)

        @pl.when(jnp.logical_or(s == 3, s == 4))
        def _():
            lax.fori_loop(2 * s - 1, 3 * s - 2, send_many, 0)

        @pl.when(s < 2 * SLAB)
        def _():
            segment(s)

        pl.when(s == 0)(pick_field)

        pl.when(s == 1)(wait_tables)
        pl.when(s == 2)(pass_field)

        @pl.when(s == 4)
        def _():
            last_fields()
            field_factors()

        here = s - SLAB * parity

        @pl.when(jnp.logical_and(here >= 2, here <= 6))
        def _():
            stage_in(here - 2)

        pl.when(here == 6)(stage_fx)
        pl.when(here == 7)(stage_zy)
        pl.when(here == 8)(stage_bx)
        return 0

    lax.fori_loop(0, 14, slot, 0)

    def back_copy(g, x):
        return remote(back.at[g, x], late.at[me, x], back_send.at[g], back_recv.at[me, x], (w, g))

    def self_back(x):
        return pltpu.make_async_copy(back.at[me, x], late.at[me, x], local_sem.at[x])

    def stage_bz(x, _):
        data = [wa[:, x, yh].reshape(320, LANES).astype(BF) for yh in range(HIGH)]
        turned_y = jnp.dot(jnp.concatenate(data, axis=1), by[...], preferred_element_type=F32).astype(BF)
        for h in range(2):
            value = jnp.dot(bz[...], turned_y[h * 160:h * 160 + 160], preferred_element_type=F32)
            for yh in range(HIGH):
                back[h * 4:h * 4 + 4, x, yh] = combined(value, yh, 160).reshape(4, G, LANES).astype(BF)
        for k in (4, 3, -3, 2, -2, 1, -1):
            back_copy(ring(k), x).start()
        self_back(x).start()
        return 0

    lax.fori_loop(0, SLAB, stage_bz, 0)

    turn_trial()

    part[...] = jnp.zeros_like(part)

    def finish(x, _):
        for k in range(1, RING):
            g = ring(k)
            remote(back.at[g, x], late.at[g, x], back_send.at[g], back_recv.at[g, x], (w, g)).wait_recv()
        self_back(x).wait()

        total = part[...]
        for yh in range(HIGH):
            moved = swap_blocks([late[d, x, yh] for d in range(RING)], lane)
            for i in range(LOW):
                out_ref[x, yh * LOW + i] = moved[i]
            new = jnp.concatenate([m.astype(F32) for m in moved], axis=0).astype(BF)
            total = total + jnp.dot(turned[x * HIGH + yh], new, preferred_element_type=F32)
        part[...] = total
        return 0

    lax.fori_loop(0, SLAB, finish, 0)

    lower = part[HALF:, :]
    mine = part[:HALF, :] - pltpu.roll(lower, HALF, 1) * sign
    parts[me] = mine.astype(BF)

    def sum_copy(d):
        return remote(parts.at[me], parts.at[me], sum_send.at[d], sum_recv.at[me], (w, d))

    for k in (4, 3, -3, 2, -2, 1, -1):
        sum_copy(ring(k)).start()

    remote(own, near, near_send, near_recv.at[0, 0], sibling).wait_send()
    near_field().wait_send()
    for k, origin in field_sends:
        ring_field(k, origin).wait_send()
    for way in range(2):
        ask(way).wait_send()
        field_copy(way).wait_send()
        remote(pre_out.at[way], pre_in.at[way], pre_send.at[way], pre_recv.at[way, 0, 0], ahead).wait_send()
    for k in range(1, RING):
        d = ring(k)
        remote(sent.at[d], got.at[me], in_send.at[d], in_recv.at[me, 0], (w, d)).wait_send()
        remote(back.at[d], late.at[me], back_send.at[d], back_recv.at[me, 0], (w, d)).wait_send()

    for k in range(1, RING):
        g = ring(k)
        remote(parts.at[g], parts.at[g], sum_send.at[g], sum_recv.at[g], (w, g)).wait_recv()
    total = parts[0].astype(F32)
    for g in range(1, RING):
        total = total + parts[g].astype(F32)
    inter_ref[...] = total * (1.0 / math.sqrt(G**3))
    for k in range(1, RING):
        sum_copy(ring(k)).wait_send()


def hand_over(walkers, inter, walkers_out, inter_out, sem):
    copies = [pltpu.make_async_copy(walkers.at[x], walkers_out.at[0, x], sem.at[x]) for x in range(SLAB)]
    copies.append(pltpu.make_async_copy(inter, inter_out.at[0], sem.at[SLAB]))
    for c in copies:
        c.start()
    for c in copies:
        c.wait()


def on_device(walkers_in, trial, fields, sources):
    made = [jnp.asarray(t) for t in tables()]
    anywhere = pl.BlockSpec(memory_space=pl.ANY)
    chunk = (SLAB, HIGH, G, LANES)
    dma = pltpu.SemaphoreType.DMA
    scratch = [
        pltpu.VMEM((SLAB, G, G, LANES), BF),
        pltpu.VMEM((SLAB, G, G, LANES), BF),
        pltpu.VMEM((SLAB * HIGH, LANES, LOW * G), BF),
        pltpu.VMEM((RING,) + chunk, BF),
        pltpu.VMEM((RING,) + chunk, BF),
        pltpu.VMEM((2, RING) + chunk, BF),
        pltpu.VMEM((2, RING) + chunk, BF),
        pltpu.VMEM((RING,) + chunk, BF),
        pltpu.VMEM((RING,) + chunk, BF),
        pltpu.VMEM((RING,) + chunk, F32),
        pltpu.VMEM((RING,) + chunk, F32),
        pltpu.VMEM((2, RING) + chunk, F32),
        pltpu.VMEM((RING,) + chunk, BF),
        pltpu.VMEM((RING,) + chunk, BF),
        pltpu.VMEM((SLAB, 2, G * G), BF),
        pltpu.VMEM((8, WIDE), BF),
        pltpu.VMEM((8, WIDE), BF),
        pltpu.VMEM((2, 8, WIDE), BF),
        pltpu.VMEM((2, 8, WIDE), BF),
        pltpu.VMEM((RING, 8, WIDE), BF),
        pltpu.VMEM((WIDE, LANES), F32),
        pltpu.VMEM((8, LANES), F32),
        pltpu.VMEM((2, 8, LANES), F32),
    ]
    scratch += [pltpu.VMEM(t.shape, BF) for t in made]
    scratch += [pltpu.VMEM((LANES, LANES), F32), pltpu.VMEM((RING, HALF, LANES), BF)]
    scratch += [
        dma((3,)), dma((SLAB,)), dma((len(made),)), dma, dma((RING, SLAB)), dma((2,)), dma((2, RING, SLAB)), dma((RING,)), dma((RING, SLAB)),
        dma((RING,)), dma((RING, SLAB)), dma, dma, dma((2,)), dma((2,)), dma((2,)), dma((2,)), dma((9,)),
        dma((RING,)), dma((RING,)), dma((RING,)), dma((SLAB,)),
    ]
    walkers_out, inter = pl.pallas_call(
        kernel,
        out_shape=(pltpu.VMEM((SLAB, G, G, LANES), BF), pltpu.VMEM((HALF, LANES), F32)),
        in_specs=[pl.BlockSpec(memory_space=pltpu.SMEM)] + [anywhere] * (3 + len(made)),
        out_specs=(pl.BlockSpec(memory_space=pltpu.VMEM),) * 2,
        scratch_shapes=scratch,
        compiler_params=pltpu.CompilerParams(
            collective_id=0, has_side_effects=True, vmem_limit_bytes=58 * 2**20
        ),
        name="walkers",
    )(sources, walkers_in, trial, fields.reshape(2, SLAB, G * G).transpose(1, 0, 2), *made)
    return pl.pallas_call(
        hand_over,
        out_shape=(
            jax.ShapeDtypeStruct((1, SLAB, G, G, LANES), BF),
            jax.ShapeDtypeStruct((1, HALF, LANES), F32),
        ),
        in_specs=[pl.BlockSpec(memory_space=pltpu.VMEM)] * 2,
        out_specs=(anywhere,) * 2,
        scratch_shapes=[dma((SLAB + 1,))],
        name="results",
    )(*(pltpu.with_memory_space_constraint(a, pltpu.VMEM) for a in (walkers_out, inter)))


def solution(mesh):
    placed = (
        P("walk", "grid", None, None, None),
        P("grid", None, None, None),
        P(None, "walk", "grid", None),
        P("walk"),
    )
    return jax.shard_map(
        on_device,
        mesh=mesh,
        in_specs=placed,
        out_specs=(P("walk", "grid", None, None, None), P("walk", None, None)),
        check_vma=False,
    )
```
